32 devices in a mesh: wide: 8 (over z, x), narrow: 4 (over y, core).
Axes of the slice: x: 2, y: 2, z: 4, core: 2. Of those that a mesh axis runs over, the one named last changes fastest.
Arguments:
- tokens: bfloat16 [512, 8192], P('wide', 'narrow'), may hold values from -6 to 6
- grad_out: bfloat16 [512, 8192], P('wide', 'narrow'), may hold values from -6 to 6
- gate_weight: bfloat16 [8192, 24576], P('narrow', 'wide'), may hold values from -0.15625 to 0.15625
- up_weight: bfloat16 [8192, 24576], P('narrow', 'wide'), may hold values from -0.15625 to 0.15625
- down_weight: bfloat16 [24576, 8192], P('wide', 'narrow'), may hold values from -0.078125 to 0.078125
- block_mask: int32 [3, 64, 192], P(None, 'narrow', 'wide'), may hold values 0 or 1
Outputs:
- output: bfloat16 [512, 8192], P('wide', 'narrow')
- input_grad: bfloat16 [512, 8192], P('wide', 'narrow')
- gate_wgrad: bfloat16 [8192, 24576], P('narrow', 'wide')
- up_wgrad: bfloat16 [8192, 24576], P('narrow', 'wide')
- down_wgrad: bfloat16 [24576, 8192], P('wide', 'narrow')
The draws below stay inside these ranges and needn't reach their ends.
All inputs are finite; a program needn't handle non-finite values. No bound on the sum of `block_mask` on one device may be relied on, other than what follows from the above.
Results may differ from the reference program's by a relative error of at most 0.0051.
Values may be sent and summed in bfloat16 or wider, within the bound.
No kernel may reach another device: no remote copies, remote signals or barrier semaphores. Data moves between devices by JAX's collectives and lax.ppermute only.
A program may use at most 256 MiB of HBM per device.

```python
import jax
import jax.numpy as jnp
from jax import lax

D = 8192
FF = 24576
BLOCK = 128
TOKENS = 512


def touch_ends(entries, own_key, least, top_value):
    spot = [jax.random.randint(jax.random.fold_in(own_key, axis), (), 0, length) for axis, length in enumerate(entries.shape)]
    longest = entries.shape.index(max(entries.shape))
    beside = spot[:longest] + [(spot[longest] + 1) % entries.shape[longest]] + spot[longest + 1:]
    return entries.at[tuple(spot)].set(least).at[tuple(beside)].set(top_value)


def levels(stream_key, dims, pieces, least, largest):
    loudness, own = 1.0, jax.random.fold_in(stream_key, 6)
    for dim, blocks in pieces:
        steps = jnp.exp(jax.random.uniform(jax.random.fold_in(own, dim), (blocks,), jnp.float32, least / len(pieces), largest / len(pieces)))
        loudness = loudness * jnp.repeat(steps, dims[dim] // blocks).reshape([-1 if axis == dim else 1 for axis in range(len(dims))])
    return loudness


def normal_values(own_key, extent, spread, limit, split=(), kind=jnp.bfloat16):
    factor_of = levels(own_key, extent, split, -0.22, 0.18) if split else 1.0
    values = jax.random.normal(own_key, extent, jnp.float32) * spread * factor_of
    return jnp.minimum(jnp.maximum(values, -limit), limit).astype(kind)


def setup_inputs(seed: int = 0) -> dict:
    splits = jax.random.split(jax.random.key(seed), 7)
    tokens = normal_values(splits[0], (TOKENS, D), 1.0, 6.0, ((0, 8), (1, 4)))
    grad_out = normal_values(splits[1], (TOKENS, D), 1.0, 6.0, ((0, 8), (1, 4)))
    gate_weight = normal_values(splits[2], (D, FF), (D // 5) ** -0.5, 0.15625, ((0, 4), (1, 8)))
    up_weight = normal_values(splits[3], (D, FF), (D // 5) ** -0.5, 0.15625, ((0, 4), (1, 8)))
    down_weight = normal_values(splits[4], (FF, D), (FF // 5) ** -0.5, 0.078125, ((0, 8), (1, 4)))
    block_mask = touch_ends((jax.random.randint(splits[5], (3, D // BLOCK, FF // BLOCK), 0, 5) < 1).astype(jnp.int32), jax.random.fold_in(splits[5], 1), 0, 1)
    return dict(tokens=tokens, grad_out=grad_out, gate_weight=gate_weight, up_weight=up_weight, down_weight=down_weight, block_mask=block_mask)


def expand_mask(blocks, height, width, dtype):
    tall = jnp.repeat(blocks, height // blocks.shape[0], axis=0)
    return jnp.repeat(tall, width // blocks.shape[1], axis=1).astype(dtype)


def contract_first(left, right):
    return lax.dot_general(left, right, (((0,), (0,)), ((), ())), preferred_element_type=jnp.float32)


def contract_last(left, right):
    return lax.dot_general(left, right, (((1,), (1,)), ((), ())), preferred_element_type=jnp.float32)


def reference(tokens, grad_out, gate_weight, up_weight, down_weight, block_mask):
    wtype = gate_weight.dtype
    mask_gate = expand_mask(block_mask[0], gate_weight.shape[0], gate_weight.shape[1], wtype)
    mask_up = expand_mask(block_mask[1], up_weight.shape[0], up_weight.shape[1], wtype)
    mask_down = expand_mask(block_mask[2].T, down_weight.shape[0], down_weight.shape[1], wtype)
    gate_masked = gate_weight * mask_gate
    up_masked = up_weight * mask_up
    down_masked = down_weight * mask_down
    gate_pre = jnp.dot(tokens, gate_masked, preferred_element_type=jnp.float32)
    up_pre = jnp.dot(tokens, up_masked, preferred_element_type=jnp.float32)
    sig = jax.nn.sigmoid(gate_pre)
    hidden = (gate_pre * sig * up_pre).astype(jnp.bfloat16)
    output = jnp.dot(hidden, down_masked, preferred_element_type=jnp.float32).astype(jnp.bfloat16)
    hidden_grad = contract_last(grad_out, down_masked)
    gate_grad = (hidden_grad * up_pre * sig * (1.0 + gate_pre * (1.0 - sig))).astype(jnp.bfloat16)
    up_grad = (hidden_grad * gate_pre * sig).astype(jnp.bfloat16)
    input_grad = (contract_last(gate_grad, gate_masked) + contract_last(up_grad, up_masked)).astype(jnp.bfloat16)
    gate_wgrad = (contract_first(tokens, gate_grad) * mask_gate).astype(jnp.bfloat16)
    up_wgrad = (contract_first(tokens, up_grad) * mask_up).astype(jnp.bfloat16)
    down_wgrad = (contract_first(hidden, grad_out) * mask_down).astype(jnp.bfloat16)
    return (output, input_grad, gate_wgrad, up_wgrad, down_wgrad)
```

```python
import functools

import jax
import jax.numpy as jnp
from jax import lax
from jax.experimental import pallas as pl
from jax.experimental.pallas import tpu as pltpu
from jax.sharding import PartitionSpec as P

F32, BF16 = jnp.float32, jnp.bfloat16
SIDE = 128
TILE = 512
CHUNKS = 4
GROUP = 8
PIECE = 8
UNROLL = 4
VMEM = 56 * 1024 * 1024


def expand_mask(blocks, height, width, dtype):
    tall = jnp.repeat(blocks, height // blocks.shape[0], axis=0)
    return jnp.repeat(tall, width // blocks.shape[1], axis=1).astype(dtype)


def contract_first(left, right):
    return lax.dot_general(
        left, right, (((0,), (0,)), ((), ())), preferred_element_type=jnp.float32
    )


def contract_last(left, right):
    return lax.dot_general(
        left, right, (((1,), (1,)), ((), ())), preferred_element_type=jnp.float32
    )


def plain_body(tokens, grad_out, gate_weight, up_weight, down_weight, block_mask):
    wtype = gate_weight.dtype
    mask_gate = expand_mask(block_mask[0], gate_weight.shape[0], gate_weight.shape[1], wtype)
    mask_up = expand_mask(block_mask[1], up_weight.shape[0], up_weight.shape[1], wtype)
    mask_down = expand_mask(block_mask[2].T, down_weight.shape[0], down_weight.shape[1], wtype)
    gate_masked = gate_weight * mask_gate
    up_masked = up_weight * mask_up
    down_masked = down_weight * mask_down
    inputs_all, cotan_all = (
        lax.all_gather(tokens, "wide", axis=0, tiled=True),
        lax.all_gather(grad_out, "wide", axis=0, tiled=True),
    )
    gate_part = jnp.dot(inputs_all, gate_masked, preferred_element_type=jnp.float32)
    up_part = jnp.dot(inputs_all, up_masked, preferred_element_type=jnp.float32)
    gate_pre, up_pre = lax.psum((gate_part, up_part), "narrow")
    sig = jax.nn.sigmoid(gate_pre)
    hidden = (gate_pre * sig * up_pre).astype(jnp.bfloat16)
    output = lax.psum_scatter(
        jnp.dot(hidden, down_masked, preferred_element_type=jnp.float32),
        "wide",
        scatter_dimension=0,
        tiled=True,
    ).astype(jnp.bfloat16)
    grad_part = contract_last(cotan_all, down_masked)
    hidden_grad = lax.psum(grad_part, "narrow")
    gate_grad = (hidden_grad * up_pre * sig * (1.0 + gate_pre * (1.0 - sig))).astype(jnp.bfloat16)
    up_grad = (hidden_grad * gate_pre * sig).astype(jnp.bfloat16)
    input_grad = lax.psum_scatter(
        contract_last(gate_grad, gate_masked) + contract_last(up_grad, up_masked),
        "wide",
        scatter_dimension=0,
        tiled=True,
    ).astype(jnp.bfloat16)
    gate_wgrad = (contract_first(inputs_all, gate_grad) * mask_gate).astype(jnp.bfloat16)
    up_wgrad = (contract_first(inputs_all, up_grad) * mask_up).astype(jnp.bfloat16)
    down_wgrad = (contract_first(hidden, cotan_all) * mask_down).astype(jnp.bfloat16)
    return (output, input_grad, gate_wgrad, up_wgrad, down_wgrad)


def tables(mask):
    count = mask.shape[1]
    kept = mask != 0
    before = jnp.arange(count)[:, None] < jnp.arange(count)[None, :]
    rank = jnp.sum(kept[:, :, None, :] & before[None, :, :, None], axis=1)
    slots = -(-count // GROUP) * GROUP
    hit = kept[:, :, None, :] & (rank[:, :, None, :] == jnp.arange(slots)[None, None, :, None])
    gap = count - jnp.arange(count)
    slot = count - jnp.sum(jnp.where(hit, gap[None, :, None, None], 0), axis=1)
    each = jnp.sum(kept, axis=1)
    wide = jnp.arange(mask.shape[2])
    ends = jnp.sum(jnp.where(wide[None, :, None] < jnp.arange(mask.shape[2] + 1)[None, None, :], each[:, :, None], 0), axis=1)
    slot = jnp.transpose(slot, (0, 2, 1)).astype(jnp.int32)
    return slot.reshape(slot.shape[0] * slot.shape[1], slots), ends.astype(jnp.int32)


def pack_kernel(slot1, ends1, slot2, ends2, gate_ref, up_ref, down_ref, *refs):
    lists, sem = refs[:6], refs[6]

    def copies(act):
        for which in range(6):
            first = which < 3
            matrix = which % 3
            slot, ends = (slot1, ends1) if first else (slot2, ends2)
            weight = (gate_ref, up_ref, down_ref)[matrix]
            columns = ends.shape[1] - 1
            straight = first == (matrix < 2)

            def column(j, carry):
                start = ends[matrix, j]

                def block(s, inner):
                    k = slot[matrix * columns + j, s]
                    row, col = (k, j) if straight else (j, k)
                    act(pltpu.make_async_copy(
                        weight.at[pl.ds(pl.multiple_of(row * SIDE, SIDE), SIDE), pl.ds(pl.multiple_of(col * SIDE, SIDE), SIDE)],
                        lists[which].at[start + s],
                        sem,
                    ))
                    return inner

                return lax.fori_loop(0, ends[matrix, j + 1] - start, block, carry)

            lax.fori_loop(0, columns, column, 0)

    copies(lambda copy: copy.start())
    copies(lambda copy: copy.wait())


def pack_blocks(weights, first, second):
    blocks = weights[0].shape[0] // SIDE * (weights[0].shape[1] // SIDE)
    shape = jax.ShapeDtypeStruct((-(-blocks // PIECE) * PIECE + PIECE, SIDE, SIDE), BF16)
    return pl.pallas_call(
        pack_kernel,
        grid_spec=pltpu.PrefetchScalarGridSpec(
            num_scalar_prefetch=4,
            grid=(1,),
            in_specs=[pl.BlockSpec(memory_space=pl.ANY)] * 3,
            out_specs=[pl.BlockSpec(memory_space=pl.ANY)] * 6,
            scratch_shapes=[pltpu.SemaphoreType.DMA(())],
        ),
        out_shape=[shape] * 6,
        cost_estimate=pl.CostEstimate(flops=0, bytes_accessed=60_000_000, transcendentals=0),
        name="pack_blocks",
    )(*first, *second, *weights)


def fetch_pieces(ends, lists, bufs, sems, act):
    for i in range(3):
        total = ends[i, ends.shape[1] - 1]

        def piece(p, carry):
            where = pl.ds(p * PIECE, PIECE)
            act(i, pltpu.make_async_copy(lists[i].at[where], bufs[i].at[where], sems.at[i]))
            return carry

        lax.fori_loop(0, (total + PIECE - 1) // PIECE, piece, 0)


def wait_pieces(ends, lists, bufs, sems, i):
    total = ends[i, ends.shape[1] - 1]

    def piece(p, carry):
        where = pl.ds(p * PIECE, PIECE)
        pltpu.make_async_copy(lists[i].at[where], bufs[i].at[where], sems.at[i]).wait()
        return carry

    lax.fori_loop(0, (total + PIECE - 1) // PIECE, piece, 0)
    bufs[i][pl.ds(total, GROUP)] = jnp.zeros((GROUP, SIDE, SIDE), BF16)


def group_dot(slot, ends, i, j, g, left, buf, straight):
    columns = ends.shape[1] - 1
    start = ends[i, j] + g * GROUP
    acts = jnp.concatenate([left[slot[i * columns + j, g * GROUP + s]] for s in range(GROUP)], axis=1)
    if straight:
        block = buf[pl.ds(start, GROUP)].reshape(GROUP * SIDE, SIDE)
        return jnp.dot(acts, block, preferred_element_type=F32)
    block = jnp.concatenate([buf[start + s] for s in range(GROUP)], axis=1)
    return contract_last(acts, block)


def more_groups(slot, ends, i, j, left, buf, straight, add):
    groups = (ends[i, j + 1] - ends[i, j] + GROUP - 1) // GROUP

    @pl.when(groups > 1)
    def _():
        def body(g, carry):
            add(group_dot(slot, ends, i, j, g, left, buf, straight))
            return carry

        lax.fori_loop(1, groups, body, 0)


def pre_kernel(core_ref, slot, ends, x_ref, g_ref, *refs):
    lists, (send_ref, keep_ref), bufs, (xs, gs, sems) = refs[:3], refs[3:5], refs[5:8], refs[8:]
    fetch_pieces(ends, lists, bufs, sems, lambda i, copy: copy.start())
    blocks = x_ref.shape[1] // SIDE
    for ref, scratch in ((x_ref, xs), (g_ref, gs)):
        for k in range(blocks):
            scratch[k] = ref[:, k * SIDE:(k + 1) * SIDE]
        scratch[blocks] = jnp.zeros(scratch.shape[1:], BF16)
    half = send_ref.shape[2] // SIDE
    core = core_ref[0]
    for i in range(3):
        wait_pieces(ends, lists, bufs, sems, i)
        left, straight = (xs, True) if i < 2 else (gs, False)
        for out, base in ((send_ref, half * (1 - core)), (keep_ref, half * core)):
            def some(t, carry):
                for u in range(UNROLL):
                    q = t * UNROLL + u
                    value = group_dot(slot, ends, i, base + q, 0, left, bufs[i], straight)
                    out[i, :, pl.ds(pl.multiple_of(q * SIDE, SIDE), SIDE)] = value
                return carry

            lax.fori_loop(0, half // UNROLL, some, 0)

            def extra(q, carry):
                def add(value):
                    out[i, :, pl.ds(pl.multiple_of(q * SIDE, SIDE), SIDE)] += value

                more_groups(slot, ends, i, base + q, left, bufs[i], straight, add)
                return carry

            lax.fori_loop(0, half, extra, 0)


def pre_partials(core, x, g, table, lists, width):
    m, depth = x.shape
    half = width // 2
    whole = pl.BlockSpec(memory_space=pltpu.VMEM)
    return pl.pallas_call(
        pre_kernel,
        grid_spec=pltpu.PrefetchScalarGridSpec(
            num_scalar_prefetch=3,
            grid=(1,),
            in_specs=[whole] * 2 + [pl.BlockSpec(memory_space=pl.ANY)] * 3,
            out_specs=[whole] * 2,
            scratch_shapes=[pltpu.VMEM(lists[0].shape, BF16)] * 3
            + [pltpu.VMEM((depth // SIDE + 1, m, SIDE), BF16)] * 2
            + [pltpu.SemaphoreType.DMA((3,))],
        ),
        out_shape=[jax.ShapeDtypeStruct((3, m, half), F32)] * 2,
        compiler_params=pltpu.CompilerParams(vmem_limit_bytes=VMEM),
        cost_estimate=pl.CostEstimate(flops=2 * m * depth * width, bytes_accessed=8_000_000, transcendentals=0),
        name="pre_partials",
    )(core, *table, x, g, *lists)


def post_kernel(core_ref, slot, ends, mine_ref, other_ref, *refs):
    lists, (keep_ref, send_ref), bufs, (hs, acc_ref, sems) = refs[:3], refs[3:5], refs[5:8], refs[8:]
    fetch_pieces(ends, lists, bufs, sems, lambda i, copy: copy.start())
    m = mine_ref.shape[1]
    half = mine_ref.shape[2] // SIDE
    core = core_ref[0]
    for i, act in enumerate((1, 2, 0)):
        for ref, base in ((mine_ref, half * core), (other_ref, half * (1 - core))):
            for k in range(half):
                hs[i, base + k] = ref[act, :, k * SIDE:(k + 1) * SIDE]
        hs[i, 2 * half] = jnp.zeros((m, SIDE), BF16)
    columns = ends.shape[1] - 1
    for i, part in ((2, 0), (0, 1), (1, 1)):
        wait_pieces(ends, lists, bufs, sems, i)
        left, straight = hs.at[i], i == 2

        def some(t, carry):
            for u in range(UNROLL):
                j = t * UNROLL + u
                where = pl.ds(pl.multiple_of(j * SIDE, SIDE), SIDE)
                value = group_dot(slot, ends, i, j, 0, left, bufs[i], straight)
                if i == 1:
                    value = value + acc_ref[part, :, where]
                acc_ref[part, :, where] = value
            return carry

        lax.fori_loop(0, columns // UNROLL, some, 0)

        def extra(j, carry):
            def add(value):
                acc_ref[part, :, pl.ds(pl.multiple_of(j * SIDE, SIDE), SIDE)] += value

            more_groups(slot, ends, i, j, left, bufs[i], straight, add)
            return carry

        lax.fori_loop(0, columns, extra, 0)
    keep_ref[...] = acc_ref[:, :m // 2]
    send_ref[...] = acc_ref[:, m // 2:].astype(BF16)


def post_partials(core, mine, other, table, lists, depth):
    m, half = mine.shape[1:]
    whole = pl.BlockSpec(memory_space=pltpu.VMEM)
    return pl.pallas_call(
        post_kernel,
        grid_spec=pltpu.PrefetchScalarGridSpec(
            num_scalar_prefetch=3,
            grid=(1,),
            in_specs=[whole] * 2 + [pl.BlockSpec(memory_space=pl.ANY)] * 3,
            out_specs=[whole] * 2,
            scratch_shapes=[pltpu.VMEM(lists[0].shape, BF16)] * 3
            + [pltpu.VMEM((3, 2 * half // SIDE + 1, m, SIDE), BF16), pltpu.VMEM((2, m, depth), F32)]
            + [pltpu.SemaphoreType.DMA((3,))],
        ),
        out_shape=[jax.ShapeDtypeStruct((2, m // 2, depth), F32), jax.ShapeDtypeStruct((2, m // 2, depth), BF16)],
        compiler_params=pltpu.CompilerParams(vmem_limit_bytes=VMEM),
        cost_estimate=pl.CostEstimate(flops=4 * m * depth * half, bytes_accessed=8_000_000, transcendentals=0),
        name="post_partials",
    )(core, *table, mine, other, *lists)


def wgrad_kernel(core_ref, *refs, chunks, steps):
    xs, gs, mines, others = (refs[i * chunks:(i + 1) * chunks] for i in range(4))
    mg_ref, mu_ref, md_ref, gate_ref, up_ref, down_ref, xt_ref, g_ref = refs[4 * chunks:]
    step = pl.program_id(0)
    m, depth = xs[0].shape

    @pl.when(step == 0)
    def _():
        for i in range(chunks):
            xt_ref[:, i * m:(i + 1) * m] = xs[i][...].T
            g_ref[i * m:(i + 1) * m, :] = gs[i][...]

    acts = jnp.concatenate([jnp.where(step < steps, a[...], b[...]) for a, b in zip(mines, others)], axis=1)
    for start in range(0, depth, TILE):
        xt = xt_ref[start:start + TILE, :]
        for act, scale, out in ((acts[1], mg_ref, gate_ref), (acts[2], mu_ref, up_ref)):
            value = jnp.dot(xt, act, preferred_element_type=F32)
            for off in range(0, TILE, SIDE):
                block = (start + off) // SIDE
                out[start + off:start + off + SIDE, :] = (value[off:off + SIDE] * scale[block:block + 1, :].astype(F32)).astype(BF16)
    value = jnp.dot(acts[0].T, g_ref[...], preferred_element_type=F32)
    for block in range(TILE // SIDE):
        rows = slice(block * SIDE, (block + 1) * SIDE)
        down_ref[rows, :] = (value[rows] * md_ref[0, block:block + 1, :].astype(F32)).astype(BF16)


def weight_grads(core, xs, gs, mines, others, masks, width):
    chunks = len(xs)
    m, depth = xs[0].shape
    steps = width // 2 // TILE
    column = lambda s, c: (s + steps * c[0]) % (2 * steps)
    spec = pltpu.PrefetchScalarGridSpec(
        num_scalar_prefetch=1,
        grid=(2 * steps,),
        in_specs=[pl.BlockSpec((m, depth), lambda s, c: (0, 0))] * (2 * chunks)
        + [pl.BlockSpec((3, m, TILE), lambda s, c: (0, 0, jnp.minimum(s, steps - 1)))] * chunks
        + [pl.BlockSpec((3, m, TILE), lambda s, c: (0, 0, jnp.maximum(s - steps, 0)))] * chunks
        + [
            pl.BlockSpec((depth // SIDE, TILE), lambda s, c: (0, column(s, c))),
            pl.BlockSpec((depth // SIDE, TILE), lambda s, c: (0, column(s, c))),
            pl.BlockSpec((1, TILE // SIDE, depth), lambda s, c: (column(s, c), 0, 0)),
        ],
        out_specs=[
            pl.BlockSpec((depth, TILE), lambda s, c: (0, column(s, c))),
            pl.BlockSpec((depth, TILE), lambda s, c: (0, column(s, c))),
            pl.BlockSpec((TILE, depth), lambda s, c: (column(s, c), 0)),
        ],
        scratch_shapes=[pltpu.VMEM((depth, chunks * m), BF16), pltpu.VMEM((chunks * m, depth), BF16)],
    )
    return pl.pallas_call(
        functools.partial(wgrad_kernel, chunks=chunks, steps=steps),
        grid_spec=spec,
        out_shape=[
            jax.ShapeDtypeStruct((depth, width), BF16),
            jax.ShapeDtypeStruct((depth, width), BF16),
            jax.ShapeDtypeStruct((width, depth), BF16),
        ],
        compiler_params=pltpu.CompilerParams(vmem_limit_bytes=VMEM),
        cost_estimate=pl.CostEstimate(
            flops=6 * chunks * m * depth * width, bytes_accessed=6 * depth * width, transcendentals=0
        ),
        name="weight_grads",
    )(core, *xs, *gs, *mines, *others, *masks)


def staged_body(tokens, grad_out, gate_weight, up_weight, down_weight, block_mask, *, wide):
    lines = wide // 2
    depth, width = gate_weight.shape
    core = (lax.axis_index("narrow") % 2).astype(jnp.int32).reshape(1)
    swap_core = [(i, i ^ 1) for i in range(4)]
    swap_y = [(i, i ^ 2) for i in range(4)]
    swap_x = [(i, i ^ 1) for i in range(wide)]
    fetch = lambda d: [((i + 2 * d) % wide, i) for i in range(wide)]
    give = lambda d: [(i, (i + 2 * d) % wide) for i in range(wide)]

    stretch = lambda blocks: jnp.repeat(blocks, SIDE, axis=1).astype(BF16)
    masks = (
        stretch(block_mask[0]),
        stretch(block_mask[1]),
        stretch(block_mask[2].T).reshape(width // TILE, TILE // SIDE, depth),
    )
    weights = (gate_weight, up_weight, down_weight)

    first = tables(jnp.stack([block_mask[0], block_mask[1], block_mask[2]]))
    second = tables(jnp.transpose(jnp.stack([block_mask[0], block_mask[1], block_mask[2]]), (0, 2, 1)))
    lists = pack_blocks(weights, first, second)

    rows = tokens.shape[0] // CHUNKS
    xs, gs = [], []
    gate = None
    for c in range(CHUNKS):
        own = jnp.stack([tokens[c * rows:(c + 1) * rows], grad_out[c * rows:(c + 1) * rows]])
        if gate is not None:
            own, gate = lax.optimization_barrier((own, gate))
        far = [lax.ppermute(own, "wide", fetch(d)) for d in range(1, lines)]
        gate = far
        if c == 0:
            line = [own] + far
            near = lax.ppermute(own, "wide", swap_x)
            rest = lax.ppermute(jnp.stack(far), "wide", swap_x)
            line = line + [near] + [rest[d] for d in range(lines - 1)]
        else:
            line = [own] + far
            rest = lax.ppermute(jnp.stack(line), "wide", swap_x)
            line = line + [rest[d] for d in range(lines)]
        xs.append(jnp.concatenate([block[0] for block in line], axis=0))
        gs.append(jnp.concatenate([block[1] for block in line], axis=0))

    sums, arrived = [], []
    for c in range(CHUNKS):
        send, keep = pre_partials(core, xs[c], gs[c], first, lists[:3], width)
        total = keep + lax.ppermute(send, "narrow", swap_core)
        sums.append(total)
        arrived.append(lax.ppermute(total.astype(BF16), "narrow", swap_y))

    mines, others, finals = [], [], []
    for c in range(CHUNKS):
        gate_pre, up_pre, hidden_grad = sums[c] + arrived[c].astype(F32)
        sig = jax.nn.sigmoid(gate_pre)
        hidden = gate_pre * sig * up_pre
        gate_grad = hidden_grad * up_pre * sig * (1.0 + gate_pre * (1.0 - sig))
        up_grad = hidden_grad * gate_pre * sig
        mine = jnp.stack([hidden, gate_grad, up_grad]).astype(BF16)
        other = lax.ppermute(mine, "narrow", swap_core)
        mines.append(mine)
        others.append(other)
        keep, send = post_partials(core, mine, other, second, lists[3:], depth)
        total = keep + lax.ppermute(send, "wide", swap_x).astype(F32)
        total = total.reshape(2, lines, rows, depth)
        final = total[:, 0]
        for d in range(1, lines):
            final = final + lax.ppermute(total[:, d].astype(BF16), "wide", give(d)).astype(F32)
        finals.append(final.astype(BF16))

    gate_wgrad, up_wgrad, down_wgrad = weight_grads(core, xs, gs, mines, others, masks, width)
    both = jnp.concatenate(finals, axis=1)
    return (both[0], both[1], gate_wgrad, up_wgrad, down_wgrad)


def solution(mesh):
    wide, narrow = mesh.shape["wide"], mesh.shape["narrow"]

    def body(*args):
        tokens, gate_weight = args[0], args[2]
        fits = narrow == 4 and wide == 8 and tokens.shape[0] % (16 * CHUNKS) == 0
        fits = fits and gate_weight.shape[1] % (2 * TILE) == 0 and gate_weight.shape[0] % TILE == 0
        return staged_body(*args, wide=wide) if fits else plain_body(*args)

    return jax.shard_map(
        body,
        mesh=mesh,
        in_specs=(
            P("wide", "narrow"),
            P("wide", "narrow"),
            P("narrow", "wide"),
            P("narrow", "wide"),
            P("wide", "narrow"),
            P(None, "narrow", "wide"),
        ),
        out_specs=(
            P("wide", "narrow"),
            P("wide", "narrow"),
            P("narrow", "wide"),
            P("narrow", "wide"),
            P("wide", "narrow"),
        ),
        check_vma=False,
    )
```

```python
import functools

import jax
import jax.numpy as jnp
from jax import lax
from jax.experimental import pallas as pl
from jax.experimental.pallas import tpu as pltpu
from jax.sharding import PartitionSpec as P

F32, BF16 = jnp.float32, jnp.bfloat16
SIDE = 128
TILE = 512
CHUNKS = 4
PRE_GROUP = 6
POST_GROUP = 8
PIECE = 8
VMEM = 34 * 1024 * 1024
RETURNS = ((0, 1), (2,), (3,))


def expand_mask(blocks, height, width, dtype):
    tall = jnp.repeat(blocks, height // blocks.shape[0], axis=0)
    return jnp.repeat(tall, width // blocks.shape[1], axis=1).astype(dtype)


def contract_first(left, right):
    return lax.dot_general(
        left, right, (((0,), (0,)), ((), ())), preferred_element_type=jnp.float32
    )


def contract_last(left, right):
    return lax.dot_general(
        left, right, (((1,), (1,)), ((), ())), preferred_element_type=jnp.float32
    )


def plain_body(tokens, grad_out, gate_weight, up_weight, down_weight, block_mask):
    wtype = gate_weight.dtype
    mask_gate = expand_mask(block_mask[0], gate_weight.shape[0], gate_weight.shape[1], wtype)
    mask_up = expand_mask(block_mask[1], up_weight.shape[0], up_weight.shape[1], wtype)
    mask_down = expand_mask(block_mask[2].T, down_weight.shape[0], down_weight.shape[1], wtype)
    gate_masked = gate_weight * mask_gate
    up_masked = up_weight * mask_up
    down_masked = down_weight * mask_down
    inputs_all, cotan_all = (
        lax.all_gather(tokens, "wide", axis=0, tiled=True),
        lax.all_gather(grad_out, "wide", axis=0, tiled=True),
    )
    gate_part = jnp.dot(inputs_all, gate_masked, preferred_element_type=jnp.float32)
    up_part = jnp.dot(inputs_all, up_masked, preferred_element_type=jnp.float32)
    gate_pre, up_pre = lax.psum((gate_part, up_part), "narrow")
    sig = jax.nn.sigmoid(gate_pre)
    hidden = (gate_pre * sig * up_pre).astype(jnp.bfloat16)
    output = lax.psum_scatter(
        jnp.dot(hidden, down_masked, preferred_element_type=jnp.float32),
        "wide",
        scatter_dimension=0,
        tiled=True,
    ).astype(jnp.bfloat16)
    grad_part = contract_last(cotan_all, down_masked)
    hidden_grad = lax.psum(grad_part, "narrow")
    gate_grad = (hidden_grad * up_pre * sig * (1.0 + gate_pre * (1.0 - sig))).astype(jnp.bfloat16)
    up_grad = (hidden_grad * gate_pre * sig).astype(jnp.bfloat16)
    input_grad = lax.psum_scatter(
        contract_last(gate_grad, gate_masked) + contract_last(up_grad, up_masked),
        "wide",
        scatter_dimension=0,
        tiled=True,
    ).astype(jnp.bfloat16)
    gate_wgrad = (contract_first(inputs_all, gate_grad) * mask_gate).astype(jnp.bfloat16)
    up_wgrad = (contract_first(inputs_all, up_grad) * mask_up).astype(jnp.bfloat16)
    down_wgrad = (contract_first(hidden, cotan_all) * mask_down).astype(jnp.bfloat16)
    return (output, input_grad, gate_wgrad, up_wgrad, down_wgrad)


def tables(mask, group):
    count, columns = mask.shape[1:]
    kept = mask != 0
    before = jnp.arange(count)[:, None] < jnp.arange(count)[None, :]
    rank = jnp.sum(kept[:, :, None, :] & before[None, :, :, None], axis=1)
    slots = -(-count // group) * group
    hit = kept[:, :, None, :] & (rank[:, :, None, :] == jnp.arange(slots)[None, None, :, None])
    gap = count - jnp.arange(count)
    slot = count - jnp.sum(jnp.where(hit, gap[None, :, None, None], 0), axis=1)
    each = jnp.sum(kept, axis=1)
    earlier = jnp.arange(columns)[None, :, None] < jnp.arange(columns + 1)[None, None, :]
    ends = jnp.sum(jnp.where(earlier, each[:, :, None], 0), axis=1)
    most = (jnp.max(each.reshape(-1, 2, columns // 2), axis=2) + group - 1) // group
    slot = jnp.transpose(slot, (0, 2, 1))
    return slot.astype(jnp.int32), ends.astype(jnp.int32), most.astype(jnp.int32)


def flatten(*parts):
    return jnp.concatenate([part.reshape(-1) for part in parts])


class Table:
    def __init__(self, ref, columns, slots):
        self.ref, self.columns, self.slots = ref, columns, slots
        self.base = 3 * columns * slots

    def slot(self, i, j, s):
        return self.ref[(i * self.columns + j) * self.slots + s]

    def end(self, i, j):
        return self.ref[self.base + i * (self.columns + 1) + j]

    def most(self, i, side):
        return self.ref[self.base + 3 * (self.columns + 1) + 2 * i + side]

    def core(self):
        return self.ref[self.base + 3 * (self.columns + 1) + 6]


def pack_kernel(table_ref, *refs, first, columns, slots):
    weights, lists, bufs, (gather_sems, write_sems) = refs[:3], refs[3:6], refs[6:9], refs[9:]
    table = Table(table_ref, columns, slots)

    def gather(i, act):
        straight = first == (i < 2)

        def column(j, carry):
            start = table.end(i, j)

            def block(s, inner):
                k = table.slot(i, j, s)
                row, col = (k, j) if straight else (j, k)
                row = pl.ds(pl.multiple_of(row * SIDE, SIDE), SIDE)
                col = pl.ds(pl.multiple_of(col * SIDE, SIDE), SIDE)
                act(pltpu.make_async_copy(weights[i].at[row, col], bufs[i].at[start + s], gather_sems.at[i]))
                return inner

            return lax.fori_loop(0, table.end(i, j + 1) - start, block, carry)

        lax.fori_loop(0, columns, column, 0)

    def write(i, act):
        def piece(p, carry):
            where = pl.ds(p * PIECE, PIECE)
            act(pltpu.make_async_copy(bufs[i].at[where], lists[i].at[where], write_sems.at[i]))
            return carry

        lax.fori_loop(0, (table.end(i, columns) + PIECE - 1) // PIECE, piece, 0)

    for i in range(3):
        gather(i, lambda copy: copy.start())
    for i in range(3):
        gather(i, lambda copy: copy.wait())
        write(i, lambda copy: copy.start())
    for i in range(3):
        write(i, lambda copy: copy.wait())


def pack_blocks(weights, table, first, group):
    deep, columns = (size // SIDE for size in weights[0].shape)
    blocks = deep * columns
    if not first:
        deep, columns = columns, deep
    shape = (-(-blocks // PIECE) * PIECE + PIECE, SIDE, SIDE)
    return pl.pallas_call(
        functools.partial(pack_kernel, first=first, columns=columns, slots=-(-deep // group) * group),
        grid_spec=pltpu.PrefetchScalarGridSpec(
            num_scalar_prefetch=1,
            grid=(1,),
            in_specs=[pl.BlockSpec(memory_space=pltpu.HBM)] * 3,
            out_specs=[pl.BlockSpec(memory_space=pltpu.HBM)] * 3,
            scratch_shapes=[pltpu.VMEM(shape, BF16)] * 3 + [pltpu.SemaphoreType.DMA((3,))] * 2,
        ),
        out_shape=[jax.ShapeDtypeStruct(shape, BF16)] * 3,
        compiler_params=pltpu.CompilerParams(vmem_limit_bytes=44 * 1024 * 1024),
        cost_estimate=pl.CostEstimate(flops=0, bytes_accessed=25_000_000, transcendentals=0),
        name="pack_blocks",
    )(table, *weights)


class Phases:
    def __init__(self, table, lists, bufs, sems, group, order):
        self.table = table
        self.lists, self.bufs, self.sems = lists, bufs, sems
        self.group, self.order = group, order
        self.half = table.columns // 2

    def copies(self, p, act):
        i, side = self.order[p]
        ring = p % len(self.bufs)
        start = self.table.end(i, side * self.half)
        total = self.table.end(i, (side + 1) * self.half) - start

        def piece(t, carry):
            act(pltpu.make_async_copy(
                self.lists[i].at[pl.ds(start + t * PIECE, PIECE)],
                self.bufs[ring].at[pl.ds(t * PIECE, PIECE)],
                self.sems.at[ring],
            ))
            return carry

        lax.fori_loop(0, (total + PIECE - 1) // PIECE, piece, 0)
        return ring, total

    def begin(self):
        for p in range(len(self.bufs)):
            self.copies(p, lambda copy: copy.start())

    def dot(self, i, j, g, first, left, buf, straight):
        group = self.group
        start = self.table.end(i, j) + g * group - first
        acts = jnp.concatenate([left[self.table.slot(i, j, g * group + s)] for s in range(group)], axis=1)
        if straight:
            block = buf[pl.ds(start, group)].reshape(group * SIDE, SIDE)
            return jnp.dot(acts, block, preferred_element_type=F32)
        block = jnp.concatenate([buf[start + s] for s in range(group)], axis=1)
        return contract_last(acts, block)

    def run(self, p, left, straight, put, add):
        i, side = self.order[p]
        ring, total = self.copies(p, lambda copy: copy.wait())
        buf = self.bufs[ring]
        buf[pl.ds(total, self.group)] = jnp.zeros((self.group, SIDE, SIDE), BF16)
        base = side * self.half
        first = self.table.end(i, base)
        for q in range(self.half):
            put(q, self.dot(i, base + q, 0, first, left, buf, straight))

        @pl.when(self.table.most(i, side) > 1)
        def _():
            def column(q, carry):
                j = base + q
                groups = (self.table.end(i, j + 1) - self.table.end(i, j) + self.group - 1) // self.group

                def more(g, inner):
                    add(q, self.dot(i, j, g, first, left, buf, straight))
                    return inner

                return lax.fori_loop(1, groups, more, carry)

            lax.fori_loop(0, self.half, column, 0)

        if p + len(self.bufs) < len(self.order):
            self.copies(p + len(self.bufs), lambda copy: copy.start())


def pre_kernel(table_ref, acts_ref, *refs):
    lists, outs, bufs, (xs, sums, sems, own_sem, out_sems) = refs[:3], refs[3:5], refs[5:8], refs[8:]
    blocks = acts_ref.shape[1]
    half = outs[0].shape[1]
    table = Table(table_ref, 2 * half, -(-blocks // PRE_GROUP) * PRE_GROUP)
    core = table.core()
    own = pltpu.make_async_copy(acts_ref, xs.at[:, pl.ds(0, blocks)], own_sem)
    own.start()
    order = [(i, 1 - core) for i in range(3)] + [(i, core) for i in range(3)]
    phases = Phases(table, lists, bufs, sems, PRE_GROUP, order)
    phases.begin()
    xs[:, blocks] = jnp.zeros((2,) + xs.shape[2:], BF16)
    own.wait()
    copies = []
    for p in range(6):
        i = p % 3
        left = xs.at[0] if i < 2 else xs.at[1]

        def put(q, value):
            sums[p, q] = value

        def add(q, value):
            sums[p, q] += value

        phases.run(p, left, i < 2, put, add)
        copies.append(pltpu.make_async_copy(sums.at[p], outs[p // 3].at[i], out_sems.at[p]))
        copies[-1].start()
    for copy in copies:
        copy.wait()


def pre_partials(acts, table, lists, width):
    _, blocks, m, _ = acts.shape
    half = width // 2 // SIDE
    anywhere = pl.BlockSpec(memory_space=pl.ANY)
    return pl.pallas_call(
        pre_kernel,
        grid_spec=pltpu.PrefetchScalarGridSpec(
            num_scalar_prefetch=1,
            grid=(1,),
            in_specs=[anywhere] + [pl.BlockSpec(memory_space=pltpu.HBM)] * 3,
            out_specs=[anywhere] * 2,
            scratch_shapes=[pltpu.VMEM((blocks * half + PIECE, SIDE, SIDE), BF16)] * 3
            + [pltpu.VMEM((2, blocks + 1, m, SIDE), BF16), pltpu.VMEM((6, half, m, SIDE), F32)]
            + [pltpu.SemaphoreType.DMA((3,)), pltpu.SemaphoreType.DMA(()), pltpu.SemaphoreType.DMA((6,))],
        ),
        out_shape=[jax.ShapeDtypeStruct((3, half, m, SIDE), F32)] * 2,
        compiler_params=pltpu.CompilerParams(vmem_limit_bytes=VMEM),
        cost_estimate=pl.CostEstimate(flops=3 * m * blocks * SIDE * width, bytes_accessed=12_000_000, transcendentals=0),
        name="pre_partials",
    )(table, acts, *lists)


def post_kernel(table_ref, mine_ref, other_ref, *refs):
    lists, (keep_ref, send_ref), bufs, (hs, acc_ref, sems, own_sems) = refs[:3], refs[3:5], refs[5:8], refs[8:]
    half, m = mine_ref.shape[1:3]
    table = Table(table_ref, keep_ref.shape[1], -(-2 * half // POST_GROUP) * POST_GROUP)
    owns = [
        pltpu.make_async_copy(ref, hs.at[:, pl.ds(n * half, half)], own_sems.at[n])
        for n, ref in enumerate((mine_ref, other_ref))
    ]
    for own in owns:
        own.start()
    order = [(2, 0), (2, 1), (0, 0), (0, 1), (1, 0), (1, 1)]
    phases = Phases(table, lists, bufs, sems, POST_GROUP, order)
    phases.begin()
    hs[:, 2 * half] = jnp.zeros((3, m, SIDE), BF16)
    for own in owns:
        own.wait()
    for p, (i, side) in enumerate(order):
        part, base = (0 if i == 2 else 1), side * phases.half

        def put(q, value):
            acc_ref[part, base + q] = value if i != 1 else acc_ref[part, base + q] + value

        def add(q, value):
            acc_ref[part, base + q] += value

        phases.run(p, hs.at[i], i == 2, put, add)
    keep_ref[...] = acc_ref[:, :, :m // 2]
    send_ref[...] = acc_ref[:, :, m // 2:].astype(BF16)


def post_partials(mine, other, table, lists, depth):
    _, half, m, _ = mine.shape
    blocks = depth // SIDE
    anywhere = pl.BlockSpec(memory_space=pl.ANY)
    return pl.pallas_call(
        post_kernel,
        grid_spec=pltpu.PrefetchScalarGridSpec(
            num_scalar_prefetch=1,
            grid=(1,),
            in_specs=[anywhere] * 2 + [pl.BlockSpec(memory_space=pltpu.HBM)] * 3,
            out_specs=[pl.BlockSpec(memory_space=pltpu.VMEM)] * 2,
            scratch_shapes=[pltpu.VMEM((blocks * half + PIECE, SIDE, SIDE), BF16)] * 3
            + [pltpu.VMEM((3, 2 * half + 1, m, SIDE), BF16), pltpu.VMEM((2, blocks, m, SIDE), F32)]
            + [pltpu.SemaphoreType.DMA((3,)), pltpu.SemaphoreType.DMA((2,))],
        ),
        out_shape=[
            jax.ShapeDtypeStruct((2, blocks, m // 2, SIDE), F32),
            jax.ShapeDtypeStruct((2, blocks, m // 2, SIDE), BF16),
        ],
        compiler_params=pltpu.CompilerParams(vmem_limit_bytes=VMEM),
        cost_estimate=pl.CostEstimate(flops=6 * m * depth * half * SIDE, bytes_accessed=12_000_000, transcendentals=0),
        name="post_partials",
    )(table, mine, other, *lists)


def lanes(ref, start, count):
    return jnp.concatenate([ref[start + k] for k in range(count)], axis=1)


def select_acts(step, steps, which, mines, others):
    parts = []
    for mine, other in zip(mines, others):
        mine = lanes(mine.at[which], 0, TILE // SIDE)
        other = lanes(other.at[which], 0, TILE // SIDE)
        parts.append(jnp.where(step < steps, mine, other))
    return jnp.concatenate(parts, axis=0)


def wgrad_kernel(core_ref, *refs, chunks, steps):
    xs, mines, others = (refs[i * chunks:(i + 1) * chunks] for i in range(3))
    mg_ref, mu_ref, gate_ref, up_ref, xt_ref = refs[3 * chunks:]
    step = pl.program_id(0)
    blocks, m, _ = xs[0].shape[1:]

    @pl.when(step == 0)
    def _():
        for i in range(chunks):
            for k in range(blocks):
                xt_ref[k * SIDE:(k + 1) * SIDE, i * m:(i + 1) * m] = xs[i][0, k].T

    acts = [select_acts(step, steps, n, mines, others) for n in range(2)]
    for start in range(0, blocks * SIDE, TILE):
        xt = xt_ref[start:start + TILE, :]
        for act, scale, out in zip(acts, (mg_ref, mu_ref), (gate_ref, up_ref)):
            value = jnp.dot(xt, act, preferred_element_type=F32)
            for off in range(0, TILE, SIDE):
                block = (start + off) // SIDE
                out[start + off:start + off + SIDE, :] = (value[off:off + SIDE] * scale[block:block + 1, :].astype(F32)).astype(BF16)


def down_kernel(core_ref, *refs, chunks, steps):
    gs, mines, others = (refs[i * chunks:(i + 1) * chunks] for i in range(3))
    md_ref, down_ref, g_ref = refs[3 * chunks:]
    step = pl.program_id(0)
    blocks, m, _ = gs[0].shape[1:]

    @pl.when(step == 0)
    def _():
        for i in range(chunks):
            g_ref[i * m:(i + 1) * m, :] = lanes(gs[i].at[0], 0, blocks)

    act = select_acts(step, steps, 0, mines, others)
    value = jnp.dot(act.T, g_ref[...], preferred_element_type=F32)
    for block in range(TILE // SIDE):
        rows = slice(block * SIDE, (block + 1) * SIDE)
        down_ref[rows, :] = (value[rows] * md_ref[0, block:block + 1, :].astype(F32)).astype(BF16)


def weight_grads(core, acts, mines, others, masks, width):
    chunks = len(acts)
    _, blocks, m, _ = acts[0].shape
    depth = blocks * SIDE
    steps = width // 2 // TILE
    per = TILE // SIDE
    column = lambda s, c: (s + steps * c[0]) % (2 * steps)
    shape = lambda *dims: jax.ShapeDtypeStruct(dims, BF16)
    params = pltpu.CompilerParams(vmem_limit_bytes=VMEM)

    def operands(source, count, place):
        mine = lambda s, c: (place, jnp.minimum(s, steps - 1), 0, 0)
        other = lambda s, c: (place, jnp.maximum(s - steps, 0), 0, 0)
        return (
            [pl.BlockSpec((1, blocks, m, SIDE), lambda s, c: (source, 0, 0, 0))] * chunks
            + [pl.BlockSpec((count, per, m, SIDE), mine)] * chunks
            + [pl.BlockSpec((count, per, m, SIDE), other)] * chunks
        )

    down = pl.pallas_call(
        functools.partial(down_kernel, chunks=chunks, steps=steps),
        grid_spec=pltpu.PrefetchScalarGridSpec(
            num_scalar_prefetch=1,
            grid=(2 * steps,),
            in_specs=operands(1, 1, 2) + [pl.BlockSpec((1, per, depth), lambda s, c: (column(s, c), 0, 0))],
            out_specs=pl.BlockSpec((TILE, depth), lambda s, c: (column(s, c), 0)),
            scratch_shapes=[pltpu.VMEM((chunks * m, depth), BF16)],
        ),
        out_shape=shape(width, depth),
        compiler_params=params,
        cost_estimate=pl.CostEstimate(flops=2 * chunks * m * depth * width, bytes_accessed=2 * depth * width, transcendentals=0),
        name="down_wgrad",
    )(core, *acts, *mines, *others, masks[2])
    panel = pl.BlockSpec((depth, TILE), lambda s, c: (0, column(s, c)))
    scale = pl.BlockSpec((blocks, TILE), lambda s, c: (0, column(s, c)))
    gate, up = pl.pallas_call(
        functools.partial(wgrad_kernel, chunks=chunks, steps=steps),
        grid_spec=pltpu.PrefetchScalarGridSpec(
            num_scalar_prefetch=1,
            grid=(2 * steps,),
            in_specs=operands(0, 2, 0) + [scale, scale],
            out_specs=[panel, panel],
            scratch_shapes=[pltpu.VMEM((depth, chunks * m), BF16)],
        ),
        out_shape=[shape(depth, width)] * 2,
        compiler_params=params,
        cost_estimate=pl.CostEstimate(flops=4 * chunks * m * depth * width, bytes_accessed=4 * depth * width, transcendentals=0),
        name="gate_up_wgrad",
    )(core, *acts, *mines, *others, *masks[:2])
    return gate, up, down


def staged_body(tokens, grad_out, gate_weight, up_weight, down_weight, block_mask, *, wide):
    lines = wide // 2
    depth, width = gate_weight.shape
    core = (lax.axis_index("narrow") % 2).astype(jnp.int32).reshape(1)
    swap_core = [(i, i ^ 1) for i in range(4)]
    swap_y = [(i, i ^ 2) for i in range(4)]
    swap_x = [(i, i ^ 1) for i in range(wide)]
    fetch = lambda d: [((i + 2 * d) % wide, i) for i in range(wide)]
    give = lambda d: [(i, (i + 2 * d) % wide) for i in range(wide)]

    stretch = lambda blocks: jnp.repeat(blocks, SIDE, axis=1).astype(BF16)
    masks = (
        stretch(block_mask[0]),
        stretch(block_mask[1]),
        stretch(block_mask[2].T).reshape(width // TILE, TILE // SIDE, depth),
    )
    weights = (gate_weight, up_weight, down_weight)

    flat = jnp.stack([block_mask[0], block_mask[1], block_mask[2]])
    first = tables(flat, PRE_GROUP)
    second = tables(jnp.transpose(flat, (0, 2, 1)), POST_GROUP)
    half = width // 2 // SIDE
    turned = jnp.where(second[0] < 2 * half, (second[0] + half * core[0]) % (2 * half), second[0])
    first = flatten(*first, core)
    pre_lists = pack_blocks(weights, first, True, PRE_GROUP)

    rows = tokens.shape[0] // CHUNKS
    blocks = depth // SIDE
    local = jnp.stack([tokens, grad_out]).reshape(2, -1, blocks, SIDE).transpose(0, 2, 1, 3)
    acts = []
    gate = None
    for c in range(CHUNKS):
        own = local[:, :, c * rows:(c + 1) * rows]
        if gate is not None:
            own, gate = lax.optimization_barrier((own, gate))
        far = [lax.ppermute(own, "wide", fetch(d)) for d in range(1, lines)]
        gate = far
        if c == 0:
            near = [lax.ppermute(own, "wide", swap_x)]
            rest = lax.ppermute(jnp.concatenate(far, axis=2), "wide", swap_x)
        else:
            near = []
            rest = lax.ppermute(jnp.concatenate([own] + far, axis=2), "wide", swap_x)
        acts.append(jnp.concatenate([own] + far + near + [rest], axis=2))

    sums, arrived = [], []
    for c in range(CHUNKS):
        if c > 0:
            acts[c], sending = lax.optimization_barrier((acts[c], sending))
        send, keep = pre_partials(acts[c], first, pre_lists, width)
        total = keep + lax.ppermute(send, "narrow", swap_core)
        sending = total.astype(BF16)
        sums.append(total)
        arrived.append(lax.ppermute(sending, "narrow", swap_y))
        if c == 0:
            table, sending = lax.optimization_barrier((flatten(*second), sending))
            post_lists = pack_blocks(weights, table, False, POST_GROUP)
    second = flatten(turned, *second[1:])

    mines, others, keeps, sends, finals = [], [], [], [], []
    for c in range(CHUNKS):
        gate_pre, up_pre, hidden_grad = sums[c] + arrived[c].astype(F32)
        sig = jax.nn.sigmoid(gate_pre)
        hidden = gate_pre * sig * up_pre
        gate_grad = hidden_grad * up_pre * sig * (1.0 + gate_pre * (1.0 - sig))
        up_grad = hidden_grad * gate_pre * sig
        mine = jnp.stack([gate_grad, up_grad, hidden]).astype(BF16)
        other = lax.ppermute(mine, "narrow", swap_core)
        mines.append(mine)
        others.append(other)
        keep, send = post_partials(mine, other, second, post_lists, depth)
        keeps.append(keep.reshape(2, blocks, lines, rows, SIDE))
        sends.append(send.reshape(2, blocks, lines, rows, SIDE))
    for group in RETURNS:
        keep = jnp.concatenate([keeps[c] for c in group], axis=3)
        send = jnp.concatenate([sends[c] for c in group], axis=3)
        total = keep + lax.ppermute(send, "wide", swap_x).astype(F32)
        final = total[:, :, 0]
        for d in range(1, lines):
            final = final + lax.ppermute(total[:, :, d].astype(BF16), "wide", give(d)).astype(F32)
        finals.append(final.astype(BF16))

    gate_wgrad, up_wgrad, down_wgrad = weight_grads(core, acts, mines, others, masks, width)
    both = jnp.concatenate(finals, axis=2).transpose(0, 2, 1, 3).reshape(2, -1, depth)
    return (both[0], both[1], gate_wgrad, up_wgrad, down_wgrad)


def solution(mesh):
    wide, narrow = mesh.shape["wide"], mesh.shape["narrow"]

    def body(*args):
        tokens, gate_weight = args[0], args[2]
        fits = narrow == 4 and wide == 8 and tokens.shape[0] % (16 * CHUNKS) == 0
        fits = fits and gate_weight.shape[1] % (2 * TILE) == 0 and gate_weight.shape[0] % TILE == 0
        return staged_body(*args, wide=wide) if fits else plain_body(*args)

    return jax.shard_map(
        body,
        mesh=mesh,
        in_specs=(
            P("wide", "narrow"),
            P("wide", "narrow"),
            P("narrow", "wide"),
            P("narrow", "wide"),
            P("wide", "narrow"),
            P(None, "narrow", "wide"),
        ),
        out_specs=(
            P("wide", "narrow"),
            P("wide", "narrow"),
            P("narrow", "wide"),
            P("narrow", "wide"),
            P("wide", "narrow"),
        ),
        check_vma=False,
    )
```

```python
import functools

import jax
import jax.numpy as jnp
from jax import lax
from jax.experimental import pallas as pl
from jax.experimental.pallas import tpu as pltpu
from jax.sharding import PartitionSpec as P

F32, BF16 = jnp.float32, jnp.bfloat16
SIDE = 128
SHARES = (4, 4, 6, 2)
PRE_GROUP = 6
POST_GROUP = 8
PIECE = 8
WGRAD_GROUPS = (4, 4, 6)
MIB = 1024 * 1024
RETURNS = ((0, 1), (2,), (3,))


def expand_mask(blocks, height, width, dtype):
    tall = jnp.repeat(blocks, height // blocks.shape[0], axis=0)
    return jnp.repeat(tall, width // blocks.shape[1], axis=1).astype(dtype)


def contract_first(left, right):
    return lax.dot_general(
        left, right, (((0,), (0,)), ((), ())), preferred_element_type=jnp.float32
    )


def contract_last(left, right):
    return lax.dot_general(
        left, right, (((1,), (1,)), ((), ())), preferred_element_type=jnp.float32
    )


def plain_body(tokens, grad_out, gate_weight, up_weight, down_weight, block_mask):
    wtype = gate_weight.dtype
    mask_gate = expand_mask(block_mask[0], gate_weight.shape[0], gate_weight.shape[1], wtype)
    mask_up = expand_mask(block_mask[1], up_weight.shape[0], up_weight.shape[1], wtype)
    mask_down = expand_mask(block_mask[2].T, down_weight.shape[0], down_weight.shape[1], wtype)
    gate_masked = gate_weight * mask_gate
    up_masked = up_weight * mask_up
    down_masked = down_weight * mask_down
    inputs_all, cotan_all = (
        lax.all_gather(tokens, "wide", axis=0, tiled=True),
        lax.all_gather(grad_out, "wide", axis=0, tiled=True),
    )
    gate_part = jnp.dot(inputs_all, gate_masked, preferred_element_type=jnp.float32)
    up_part = jnp.dot(inputs_all, up_masked, preferred_element_type=jnp.float32)
    gate_pre, up_pre = lax.psum((gate_part, up_part), "narrow")
    sig = jax.nn.sigmoid(gate_pre)
    hidden = (gate_pre * sig * up_pre).astype(jnp.bfloat16)
    output = lax.psum_scatter(
        jnp.dot(hidden, down_masked, preferred_element_type=jnp.float32),
        "wide",
        scatter_dimension=0,
        tiled=True,
    ).astype(jnp.bfloat16)
    grad_part = contract_last(cotan_all, down_masked)
    hidden_grad = lax.psum(grad_part, "narrow")
    gate_grad = (hidden_grad * up_pre * sig * (1.0 + gate_pre * (1.0 - sig))).astype(jnp.bfloat16)
    up_grad = (hidden_grad * gate_pre * sig).astype(jnp.bfloat16)
    input_grad = lax.psum_scatter(
        contract_last(gate_grad, gate_masked) + contract_last(up_grad, up_masked),
        "wide",
        scatter_dimension=0,
        tiled=True,
    ).astype(jnp.bfloat16)
    gate_wgrad = (contract_first(inputs_all, gate_grad) * mask_gate).astype(jnp.bfloat16)
    up_wgrad = (contract_first(inputs_all, up_grad) * mask_up).astype(jnp.bfloat16)
    down_wgrad = (contract_first(hidden, cotan_all) * mask_down).astype(jnp.bfloat16)
    return (output, input_grad, gate_wgrad, up_wgrad, down_wgrad)


def tables(mask, group):
    count, columns = mask.shape[1:]
    kept = mask != 0
    before = jnp.arange(count)[:, None] < jnp.arange(count)[None, :]
    rank = jnp.sum(kept[:, :, None, :] & before[None, :, :, None], axis=1)
    slots = -(-count // group) * group
    hit = kept[:, :, None, :] & (rank[:, :, None, :] == jnp.arange(slots)[None, None, :, None])
    gap = count - jnp.arange(count)
    slot = count - jnp.sum(jnp.where(hit, gap[None, :, None, None], 0), axis=1)
    each = jnp.sum(kept, axis=1)
    earlier = jnp.arange(columns)[None, :, None] < jnp.arange(columns + 1)[None, None, :]
    ends = jnp.sum(jnp.where(earlier, each[:, :, None], 0), axis=1)
    most = (jnp.max(each.reshape(-1, 2, columns // 2), axis=2) + group - 1) // group
    slot = jnp.transpose(slot, (0, 2, 1))
    return slot.astype(jnp.int32), ends.astype(jnp.int32), most.astype(jnp.int32)


def flatten(*parts):
    return jnp.concatenate([part.reshape(-1) for part in parts])


class Table:
    def __init__(self, ref, columns, slots):
        self.ref, self.columns, self.slots = ref, columns, slots
        self.base = 3 * columns * slots

    def slot(self, i, j, s):
        return self.ref[(i * self.columns + j) * self.slots + s]

    def end(self, i, j):
        return self.ref[self.base + i * (self.columns + 1) + j]

    def most(self, i, side):
        return self.ref[self.base + 3 * (self.columns + 1) + 2 * i + side]

    def core(self):
        return self.ref[self.base + 3 * (self.columns + 1) + 6]


def pack_kernel(table_ref, *refs, first, columns, slots):
    weights, rest = refs[:3], refs[3:]
    lists, blanks, rest = rest[0], rest[1:4 if first else 1], rest[4 if first else 1:]
    bufs, gather_sems, write_sems = rest[:3], rest[3], rest[4]
    if first:
        zeros_wide, zeros_tall, blank_sem = rest[5:]
    table = Table(table_ref, columns, slots)
    fills = []
    for blank in blanks:
        zeros = zeros_wide if blank.shape[1] == zeros_wide.shape[1] else zeros_tall
        deep = zeros.shape[0]
        for start in range(0, blank.shape[0], deep):
            fills.append(pltpu.make_async_copy(zeros, blank.at[pl.ds(start, deep)], blank_sem))
    if first:
        zeros_wide[...] = jnp.zeros(zeros_wide.shape, BF16)
        zeros_tall[...] = jnp.zeros(zeros_tall.shape, BF16)

    def gather(i, act):
        straight = first == (i < 2)

        def column(j, carry):
            start = table.end(i, j)

            def block(t, inner):
                k = table.slot(i, j, t)
                row, col = (k, j) if straight else (j, k)
                row = pl.ds(pl.multiple_of(row * SIDE, SIDE), SIDE)
                col = pl.ds(pl.multiple_of(col * SIDE, SIDE), SIDE)
                act(pltpu.make_async_copy(weights[i].at[row, col], bufs[i].at[start + t], gather_sems.at[i]))
                return inner

            return lax.fori_loop(0, table.end(i, j + 1) - start, block, carry)

        lax.fori_loop(0, columns, column, 0)

    def write(i, act):
        def piece(t, carry):
            where = pl.ds(t * PIECE, PIECE)
            act(pltpu.make_async_copy(bufs[i].at[where], lists.at[i, where], write_sems.at[i]))
            return carry

        lax.fori_loop(0, (table.end(i, columns) + PIECE - 1) // PIECE, piece, 0)

    for i in range(3):
        gather(i, lambda copy: copy.start())
    for fill in fills:
        fill.start()
    for i in range(3):
        gather(i, lambda copy: copy.wait())
        write(i, lambda copy: copy.start())
    for i in range(3):
        write(i, lambda copy: copy.wait())
    for fill in fills:
        fill.wait()


def pack_blocks(weights, table, first, group):
    deep, columns = (size // SIDE for size in weights[0].shape)
    blocks = deep * columns
    if not first:
        deep, columns = columns, deep
    shape = (-(-blocks // PIECE) * PIECE + PIECE, SIDE, SIDE)
    hbm = pl.BlockSpec(memory_space=pltpu.HBM)
    blanks = [jax.ShapeDtypeStruct(weight.shape, BF16) for weight in weights] if first else []
    zeros = [pltpu.VMEM((weight.shape[0] // 8, weight.shape[1]), BF16) for weight in weights[1:]] if first else []
    return pl.pallas_call(
        functools.partial(pack_kernel, first=first, columns=columns, slots=-(-deep // group) * group),
        grid_spec=pltpu.PrefetchScalarGridSpec(
            num_scalar_prefetch=1,
            grid=(1,),
            in_specs=[hbm] * 3,
            out_specs=[hbm] * (1 + len(blanks)),
            scratch_shapes=[pltpu.VMEM(shape, BF16)] * 3
            + [pltpu.SemaphoreType.DMA((3,))] * 2
            + zeros
            + [pltpu.SemaphoreType.DMA(())] * first,
        ),
        out_shape=[jax.ShapeDtypeStruct((3,) + shape, BF16)] + blanks,
        compiler_params=pltpu.CompilerParams(vmem_limit_bytes=48 * MIB),
        cost_estimate=pl.CostEstimate(flops=0, bytes_accessed=30_000_000, transcendentals=0),
        name="pack_blocks",
    )(table, *weights)


class Phases:
    def __init__(self, table, lists, bufs, sems, group, order):
        self.table = table
        self.lists, self.bufs, self.sems = lists, bufs, sems
        self.group, self.order = group, order
        self.half = table.columns // 2

    def copies(self, p, act):
        i, side = self.order[p]
        ring = p % len(self.bufs)
        start = self.table.end(i, side * self.half)
        total = self.table.end(i, (side + 1) * self.half) - start

        def piece(t, carry):
            act(pltpu.make_async_copy(
                self.lists.at[i, pl.ds(start + t * PIECE, PIECE)],
                self.bufs[ring].at[pl.ds(t * PIECE, PIECE)],
                self.sems.at[ring],
            ))
            return carry

        lax.fori_loop(0, (total + PIECE - 1) // PIECE, piece, 0)
        return ring, total

    def begin(self):
        for p in range(len(self.bufs)):
            self.copies(p, lambda copy: copy.start())

    def dot(self, i, j, g, first, left, buf, straight):
        group = self.group
        start = self.table.end(i, j) + g * group - first
        acts = jnp.concatenate([left[self.table.slot(i, j, g * group + s)] for s in range(group)], axis=1)
        if straight:
            block = buf[pl.ds(start, group)].reshape(group * SIDE, SIDE)
            return jnp.dot(acts, block, preferred_element_type=F32)
        block = jnp.concatenate([buf[start + s] for s in range(group)], axis=1)
        return contract_last(acts, block)

    def run(self, p, left, straight, put, add):
        i, side = self.order[p]
        ring, total = self.copies(p, lambda copy: copy.wait())
        buf = self.bufs[ring]
        buf[pl.ds(total, self.group)] = jnp.zeros((self.group, SIDE, SIDE), BF16)
        base = side * self.half
        first = self.table.end(i, base)
        for q in range(self.half):
            put(q, self.dot(i, base + q, 0, first, left, buf, straight))

        @pl.when(self.table.most(i, side) > 1)
        def _():
            def column(q, carry):
                j = base + q
                groups = (self.table.end(i, j + 1) - self.table.end(i, j) + self.group - 1) // self.group

                def more(g, inner):
                    add(q, self.dot(i, j, g, first, left, buf, straight))
                    return inner

                return lax.fori_loop(1, groups, more, carry)

            lax.fori_loop(0, self.half, column, 0)

        if p + len(self.bufs) < len(self.order):
            self.copies(p + len(self.bufs), lambda copy: copy.start())


def pre_kernel(table_ref, acts_ref, lists, *refs, after):
    refs = refs[after:]
    outs, bufs, (xs, sums, sems, own_sem, out_sems) = refs[:2], refs[2:5], refs[5:]
    blocks = acts_ref.shape[1]
    half = outs[0].shape[1]
    table = Table(table_ref, 2 * half, -(-blocks // PRE_GROUP) * PRE_GROUP)
    core = table.core()
    own = pltpu.make_async_copy(acts_ref, xs.at[:, pl.ds(0, blocks)], own_sem)
    own.start()
    order = [(i, 1 - core) for i in range(3)] + [(i, core) for i in range(3)]
    phases = Phases(table, lists, bufs, sems, PRE_GROUP, order)
    phases.begin()
    xs[:, blocks] = jnp.zeros((2,) + xs.shape[2:], BF16)
    own.wait()
    copies = []
    for p in range(6):
        i = p % 3
        left = xs.at[0] if i < 2 else xs.at[1]

        def put(q, value):
            sums[p, q] = value

        def add(q, value):
            sums[p, q] += value

        phases.run(p, left, i < 2, put, add)
        copies.append(pltpu.make_async_copy(sums.at[p], outs[p // 3].at[i], out_sems.at[p]))
        copies[-1].start()
    for copy in copies:
        copy.wait()


def pre_partials(acts, table, lists, width, after):
    _, blocks, m, _ = acts.shape
    half = width // 2 // SIDE
    anywhere = pl.BlockSpec(memory_space=pl.ANY)
    return pl.pallas_call(
        functools.partial(pre_kernel, after=len(after)),
        grid_spec=pltpu.PrefetchScalarGridSpec(
            num_scalar_prefetch=1,
            grid=(1,),
            in_specs=[anywhere, pl.BlockSpec(memory_space=pltpu.HBM)] + [anywhere] * len(after),
            out_specs=[anywhere] * 2,
            scratch_shapes=[pltpu.VMEM((blocks * half + PIECE, SIDE, SIDE), BF16)] * 3
            + [pltpu.VMEM((2, blocks + 1, m, SIDE), BF16), pltpu.VMEM((6, half, m, SIDE), F32)]
            + [pltpu.SemaphoreType.DMA((3,)), pltpu.SemaphoreType.DMA(()), pltpu.SemaphoreType.DMA((6,))],
        ),
        out_shape=[jax.ShapeDtypeStruct((3, half, m, SIDE), F32)] * 2,
        compiler_params=pltpu.CompilerParams(vmem_limit_bytes=40 * MIB),
        cost_estimate=pl.CostEstimate(flops=3 * m * blocks * SIDE * width, bytes_accessed=12_000_000, transcendentals=0),
        name="pre_partials",
    )(table, acts, lists, *after)


def post_kernel(table_ref, mine_ref, other_ref, lists, *refs, after):
    refs = refs[after:]
    (keep_ref, send_ref), bufs, (hs, acc_ref, sems, own_sems) = refs[:2], refs[2:5], refs[5:]
    half, m = mine_ref.shape[1:3]
    table = Table(table_ref, keep_ref.shape[1], -(-2 * half // POST_GROUP) * POST_GROUP)
    owns = [
        pltpu.make_async_copy(ref, hs.at[:, pl.ds(n * half, half)], own_sems.at[n])
        for n, ref in enumerate((mine_ref, other_ref))
    ]
    for own in owns:
        own.start()
    order = [(2, 0), (2, 1), (0, 0), (0, 1), (1, 0), (1, 1)]
    phases = Phases(table, lists, bufs, sems, POST_GROUP, order)
    phases.begin()
    hs[:, 2 * half] = jnp.zeros((3, m, SIDE), BF16)
    for own in owns:
        own.wait()
    for p, (i, side) in enumerate(order):
        part, base = (0 if i == 2 else 1), side * phases.half

        def put(q, value):
            acc_ref[part, base + q] = value if i != 1 else acc_ref[part, base + q] + value

        def add(q, value):
            acc_ref[part, base + q] += value

        phases.run(p, hs.at[i], i == 2, put, add)
    keep_ref[...] = acc_ref[:, :, :m // 2]
    send_ref[...] = acc_ref[:, :, m // 2:].astype(BF16)


def post_partials(mine, other, table, lists, depth, after):
    _, half, m, _ = mine.shape
    blocks = depth // SIDE
    anywhere = pl.BlockSpec(memory_space=pl.ANY)
    return pl.pallas_call(
        functools.partial(post_kernel, after=len(after)),
        grid_spec=pltpu.PrefetchScalarGridSpec(
            num_scalar_prefetch=1,
            grid=(1,),
            in_specs=[anywhere] * 2 + [pl.BlockSpec(memory_space=pltpu.HBM)] + [anywhere] * len(after),
            out_specs=[pl.BlockSpec(memory_space=pltpu.VMEM)] * 2,
            scratch_shapes=[pltpu.VMEM((blocks * half + PIECE, SIDE, SIDE), BF16)] * 3
            + [pltpu.VMEM((3, 2 * half + 1, m, SIDE), BF16), pltpu.VMEM((2, blocks, m, SIDE), F32)]
            + [pltpu.SemaphoreType.DMA((3,)), pltpu.SemaphoreType.DMA((2,))],
        ),
        out_shape=[
            jax.ShapeDtypeStruct((2, blocks, m // 2, SIDE), F32),
            jax.ShapeDtypeStruct((2, blocks, m // 2, SIDE), BF16),
        ],
        compiler_params=pltpu.CompilerParams(vmem_limit_bytes=40 * MIB),
        cost_estimate=pl.CostEstimate(flops=6 * m * depth * half * SIDE, bytes_accessed=12_000_000, transcendentals=0),
        name="post_partials",
    )(table, mine, other, lists, *after)


def wgrad_kernel(first_ref, second_ref, *refs, rows, after):
    n = len(rows)
    acts, mines, others, refs = refs[:n], refs[n:2 * n], refs[2 * n:3 * n], refs[3 * n + 3 + after:]
    outs, (xg, hs, xt, ht, *bufs, in_sems, out_sems) = refs[:3], refs[3:]
    blocks, halves = xg.shape[1], hs.shape[1]
    half = halves // 2
    pre = Table(first_ref, halves, -(-blocks // PRE_GROUP) * PRE_GROUP)
    post = Table(second_ref, blocks, -(-halves // POST_GROUP) * POST_GROUP)
    core = pre.core()
    loads, start = ([], []), 0
    for c in range(n):
        span = pl.ds(start, rows[c])
        loads[0].append(pltpu.make_async_copy(acts[c], xg.at[:, :, span], in_sems.at[0]))
        for ref, base in ((mines[c], 0), (others[c], half)):
            loads[1].append(pltpu.make_async_copy(ref, hs.at[:, pl.ds(base, half), span], in_sems.at[1]))
        start += rows[c]
    for load in loads[0] + loads[1]:
        load.start()
    for load in loads[0]:
        load.wait()
    for k in range(blocks):
        xt[k] = xg[0, k].T
    xt[blocks] = jnp.zeros(xt.shape[1:], BF16)
    for load in loads[1]:
        load.wait()
    turn = lambda k: lax.rem(k + half * core, halves)

    def stores(i, side, act):
        table = pre if i < 2 else post
        width = table.columns // 2

        def column(q, carry):
            j = side * width + q
            first = table.end(i, j)

            def block(t, inner):
                k = table.slot(i, j, t)
                k = k if i < 2 else turn(k)
                row = pl.ds(pl.multiple_of(k * SIDE, SIDE), SIDE)
                col = pl.ds(pl.multiple_of(j * SIDE, SIDE), SIDE)
                act(pltpu.make_async_copy(bufs[i % 2].at[first + t], outs[i].at[row, col], out_sems.at[i]))
                return inner

            return lax.fori_loop(0, table.end(i, j + 1) - first, block, carry)

        lax.fori_loop(0, width, column, 0)

    for i in range(3):
        table, left, group = (pre, xt, WGRAD_GROUPS[i]) if i < 2 else (post, ht, WGRAD_GROUPS[i])
        buf = bufs[i % 2]
        width = table.columns // 2
        if i == 2:
            for k in range(halves):
                ht[k] = hs[2, k].T
            ht[halves] = jnp.zeros(ht.shape[1:], BF16)
            for side in range(2):
                stores(0, side, lambda copy: copy.wait())

        def product(j, g):
            rows_of = jnp.concatenate([left[table.slot(i, j, g * group + t)] for t in range(group)], axis=0)
            right = hs[i, turn(j)] if i < 2 else xg[1, j]
            value = jnp.dot(rows_of, right, preferred_element_type=F32).astype(BF16)
            buf[pl.ds(table.end(i, j) + g * group, group)] = value.reshape(group, SIDE, SIDE)

        for side in range(2):
            def column(q, carry):
                j = side * width + q
                groups = (table.end(i, j + 1) - table.end(i, j) + group - 1) // group

                def more(g, inner):
                    product(j, g)
                    return inner

                return lax.fori_loop(1, groups, more, carry)

            lax.fori_loop(0, width, column, 0)
            for q in range(width):
                product(side * width + q, 0)
            stores(i, side, lambda copy: copy.start())
    for i in (1, 2):
        for side in range(2):
            stores(i, side, lambda copy: copy.wait())


def weight_grads(first, second, acts, mines, others, blanks, after):
    rows = [act.shape[2] for act in acts]
    tokens, blocks, halves = sum(rows), acts[0].shape[1], 2 * mines[0].shape[1]
    lists = (-(-blocks * halves // PIECE) * PIECE + PIECE, SIDE, SIDE)
    anywhere, hbm = pl.BlockSpec(memory_space=pl.ANY), pl.BlockSpec(memory_space=pltpu.HBM)
    n = len(acts)
    return pl.pallas_call(
        functools.partial(wgrad_kernel, rows=rows, after=len(after)),
        grid_spec=pltpu.PrefetchScalarGridSpec(
            num_scalar_prefetch=2,
            grid=(1,),
            in_specs=[anywhere] * (3 * n) + [hbm] * 3 + [anywhere] * len(after),
            out_specs=[hbm] * 3,
            scratch_shapes=[
                pltpu.VMEM((2, blocks, tokens, SIDE), BF16),
                pltpu.VMEM((3, halves, tokens, SIDE), BF16),
                pltpu.VMEM((blocks + 1, SIDE, tokens), BF16),
                pltpu.VMEM((halves + 1, SIDE, tokens), BF16),
                pltpu.VMEM(lists, BF16),
                pltpu.VMEM(lists, BF16),
                pltpu.SemaphoreType.DMA((2,)),
                pltpu.SemaphoreType.DMA((3,)),
            ],
        ),
        out_shape=[jax.ShapeDtypeStruct(blank.shape, BF16) for blank in blanks],
        input_output_aliases={2 + 3 * n + i: i for i in range(3)},
        compiler_params=pltpu.CompilerParams(vmem_limit_bytes=52 * MIB),
        cost_estimate=pl.CostEstimate(flops=10_000_000_000, bytes_accessed=20_000_000, transcendentals=0),
        name="weight_grads",
    )(first, second, *acts, *mines, *others, *blanks, *after)


def staged_body(tokens, grad_out, gate_weight, up_weight, down_weight, block_mask, *, wide):
    lines = wide // 2
    depth, width = gate_weight.shape
    core = (lax.axis_index("narrow") % 2).astype(jnp.int32).reshape(1)
    swap_core = [(i, i ^ 1) for i in range(4)]
    swap_y = [(i, i ^ 2) for i in range(4)]
    swap_x = [(i, i ^ 1) for i in range(wide)]
    fetch = lambda d: [((i + 2 * d) % wide, i) for i in range(wide)]
    give = lambda d: [(i, (i + 2 * d) % wide) for i in range(wide)]

    weights = (gate_weight, up_weight, down_weight)
    flat = jnp.stack([block_mask[0], block_mask[1], block_mask[2]])
    first = tables(flat, PRE_GROUP)
    second = tables(jnp.transpose(flat, (0, 2, 1)), POST_GROUP)
    half = width // 2 // SIDE
    turned = jnp.where(second[0] < 2 * half, (second[0] + half * core[0]) % (2 * half), second[0])
    first = flatten(*first, core)
    pre_lists, *blanks = pack_blocks(weights, first, True, PRE_GROUP)
    (post_lists,) = pack_blocks(weights, flatten(*second, core), False, POST_GROUP)
    second = flatten(turned, *second[1:], core)

    unit = tokens.shape[0] // sum(SHARES)
    rows = [share * unit for share in SHARES]
    blocks = depth // SIDE
    local = jnp.stack([tokens, grad_out]).reshape(2, -1, blocks, SIDE).transpose(0, 2, 1, 3)
    acts = []
    gate = None
    for c, count in enumerate(rows):
        own = local[:, :, sum(rows[:c]):sum(rows[:c]) + count]
        if gate is not None:
            own, gate = lax.optimization_barrier((own, gate))
        far = [lax.ppermute(own, "wide", fetch(d)) for d in range(1, lines)]
        gate = far
        if c == 0:
            near = [lax.ppermute(own, "wide", swap_x)]
            rest = lax.ppermute(jnp.concatenate(far, axis=2), "wide", swap_x)
        else:
            near = []
            rest = lax.ppermute(jnp.concatenate([own] + far, axis=2), "wide", swap_x)
        acts.append(jnp.concatenate([own] + far + near + [rest], axis=2))

    count = len(rows)
    sums, arrived, sending = [None] * count, [None] * count, [None] * count
    mines, others, keeps, sends = [None] * count, [None] * count, [None] * count, [None] * count

    def before(c, after):
        send, keep = pre_partials(acts[c], first, pre_lists, width, after)
        sums[c] = keep + lax.ppermute(send, "narrow", swap_core)
        sending[c] = sums[c].astype(BF16)
        arrived[c] = lax.ppermute(sending[c], "narrow", swap_y)

    def between(c):
        gate_pre, up_pre, hidden_grad = sums[c] + arrived[c].astype(F32)
        sig = jax.nn.sigmoid(gate_pre)
        hidden = gate_pre * sig * up_pre
        gate_grad = hidden_grad * up_pre * sig * (1.0 + gate_pre * (1.0 - sig))
        up_grad = hidden_grad * gate_pre * sig
        mines[c] = jnp.stack([gate_grad, up_grad, hidden]).astype(BF16)
        others[c] = lax.ppermute(mines[c], "narrow", swap_core)

    def behind(c, after):
        keep, send = post_partials(mines[c], others[c], second, post_lists, depth, after)
        keeps[c] = keep.reshape(2, blocks, lines, rows[c], SIDE)
        sends[c] = send.reshape(2, blocks, lines, rows[c], SIDE)

    def give_back(group):
        keep = jnp.concatenate([keeps[c] for c in group], axis=3)
        send = jnp.concatenate([sends[c] for c in group], axis=3)
        total = keep + lax.ppermute(send, "wide", swap_x).astype(F32)
        final = total[:, :, 0]
        for d in range(1, lines):
            final = final + lax.ppermute(total[:, :, d].astype(BF16), "wide", give(d)).astype(F32)
        return final.astype(BF16)

    before(0, [post_lists])
    before(1, [sending[0]])
    before(2, [sending[1]])
    between(0)
    before(3, [sending[2], mines[0]])
    behind(0, [sending[3]])
    between(1)
    behind(1, [keeps[0]])
    between(2)
    behind(2, [keeps[1]])
    between(3)
    behind(3, [keeps[2]])
    gate_wgrad, up_wgrad, down_wgrad = weight_grads(first, second, acts, mines, others, blanks, [keeps[3]])
    finals = [give_back(group) for group in RETURNS]
    both = jnp.concatenate(finals, axis=2).transpose(0, 2, 1, 3).reshape(2, -1, depth)
    return (both[0], both[1], gate_wgrad, up_wgrad, down_wgrad)


def solution(mesh):
    wide, narrow = mesh.shape["wide"], mesh.shape["narrow"]

    def body(*args):
        tokens, gate_weight = args[0], args[2]
        fits = narrow == 4 and wide == 8 and tokens.shape[0] % (4 * sum(SHARES)) == 0
        fits = fits and gate_weight.shape[1] % (4 * SIDE) == 0 and gate_weight.shape[0] % (2 * SIDE) == 0
        return staged_body(*args, wide=wide) if fits else plain_body(*args)

    return jax.shard_map(
        body,
        mesh=mesh,
        in_specs=(
            P("wide", "narrow"),
            P("wide", "narrow"),
            P("narrow", "wide"),
            P("narrow", "wide"),
            P("wide", "narrow"),
            P(None, "narrow", "wide"),
        ),
        out_specs=(
            P("wide", "narrow"),
            P("wide", "narrow"),
            P("narrow", "wide"),
            P("narrow", "wide"),
            P("wide", "narrow"),
        ),
        check_vma=False,
    )
```

```python
import functools

import jax
import jax.numpy as jnp
from jax import lax
from jax.experimental import pallas as pl
from jax.experimental.pallas import tpu as pltpu
from jax.sharding import PartitionSpec as P

F32, BF16 = jnp.float32, jnp.bfloat16
SIDE = 128
SHARES = (4, 4, 6, 2)
PRE_GROUP = 6
POST_GROUP = 8
PIECE = 8
WGRAD_GROUPS = (6, 6, 8)
PANEL = 4
MIB = 1024 * 1024
BRIEF = pl.CostEstimate(flops=1000, bytes_accessed=1000, transcendentals=0)
RETURNS = ((0, 1), (2,), (3,))


def expand_mask(blocks, height, width, dtype):
    tall = jnp.repeat(blocks, height // blocks.shape[0], axis=0)
    return jnp.repeat(tall, width // blocks.shape[1], axis=1).astype(dtype)


def contract_first(left, right):
    return lax.dot_general(
        left, right, (((0,), (0,)), ((), ())), preferred_element_type=jnp.float32
    )


def contract_last(left, right):
    return lax.dot_general(
        left, right, (((1,), (1,)), ((), ())), preferred_element_type=jnp.float32
    )


def plain_body(tokens, grad_out, gate_weight, up_weight, down_weight, block_mask):
    wtype = gate_weight.dtype
    mask_gate = expand_mask(block_mask[0], gate_weight.shape[0], gate_weight.shape[1], wtype)
    mask_up = expand_mask(block_mask[1], up_weight.shape[0], up_weight.shape[1], wtype)
    mask_down = expand_mask(block_mask[2].T, down_weight.shape[0], down_weight.shape[1], wtype)
    gate_masked = gate_weight * mask_gate
    up_masked = up_weight * mask_up
    down_masked = down_weight * mask_down
    inputs_all, cotan_all = (
        lax.all_gather(tokens, "wide", axis=0, tiled=True),
        lax.all_gather(grad_out, "wide", axis=0, tiled=True),
    )
    gate_part = jnp.dot(inputs_all, gate_masked, preferred_element_type=jnp.float32)
    up_part = jnp.dot(inputs_all, up_masked, preferred_element_type=jnp.float32)
    gate_pre, up_pre = lax.psum((gate_part, up_part), "narrow")
    sig = jax.nn.sigmoid(gate_pre)
    hidden = (gate_pre * sig * up_pre).astype(jnp.bfloat16)
    output = lax.psum_scatter(
        jnp.dot(hidden, down_masked, preferred_element_type=jnp.float32),
        "wide",
        scatter_dimension=0,
        tiled=True,
    ).astype(jnp.bfloat16)
    grad_part = contract_last(cotan_all, down_masked)
    hidden_grad = lax.psum(grad_part, "narrow")
    gate_grad = (hidden_grad * up_pre * sig * (1.0 + gate_pre * (1.0 - sig))).astype(jnp.bfloat16)
    up_grad = (hidden_grad * gate_pre * sig).astype(jnp.bfloat16)
    input_grad = lax.psum_scatter(
        contract_last(gate_grad, gate_masked) + contract_last(up_grad, up_masked),
        "wide",
        scatter_dimension=0,
        tiled=True,
    ).astype(jnp.bfloat16)
    gate_wgrad = (contract_first(inputs_all, gate_grad) * mask_gate).astype(jnp.bfloat16)
    up_wgrad = (contract_first(inputs_all, up_grad) * mask_up).astype(jnp.bfloat16)
    down_wgrad = (contract_first(hidden, cotan_all) * mask_down).astype(jnp.bfloat16)
    return (output, input_grad, gate_wgrad, up_wgrad, down_wgrad)


def tables(mask, group):
    count, columns = mask.shape[1:]
    kept = mask != 0
    before = jnp.arange(count)[:, None] < jnp.arange(count)[None, :]
    rank = jnp.sum(kept[:, :, None, :] & before[None, :, :, None], axis=1)
    slots = -(-count // group) * group
    hit = kept[:, :, None, :] & (rank[:, :, None, :] == jnp.arange(slots)[None, None, :, None])
    gap = count - jnp.arange(count)
    slot = count - jnp.sum(jnp.where(hit, gap[None, :, None, None], 0), axis=1)
    each = jnp.sum(kept, axis=1)
    earlier = jnp.arange(columns)[None, :, None] < jnp.arange(columns + 1)[None, None, :]
    ends = jnp.sum(jnp.where(earlier, each[:, :, None], 0), axis=1)
    most = (jnp.max(each.reshape(-1, 2, columns // 2), axis=2) + group - 1) // group
    slot = jnp.transpose(slot, (0, 2, 1))
    return slot.astype(jnp.int32), ends.astype(jnp.int32), most.astype(jnp.int32)


def flatten(*parts):
    return jnp.concatenate([part.reshape(-1) for part in parts])


class Table:
    def __init__(self, ref, columns, slots):
        self.ref, self.columns, self.slots = ref, columns, slots
        self.base = 3 * columns * slots

    def slot(self, i, j, s):
        return self.ref[(i * self.columns + j) * self.slots + s]

    def end(self, i, j):
        return self.ref[self.base + i * (self.columns + 1) + j]

    def most(self, i, side):
        return self.ref[self.base + 3 * (self.columns + 1) + 2 * i + side]

    def core(self):
        return self.ref[self.base + 3 * (self.columns + 1) + 6]


def pack_kernel(table_ref, *refs, first, columns, slots, after):
    weights, refs = refs[:3], refs[3 + after:]
    lists, bufs, (gather_sems, write_sems) = refs[0], refs[1:4], refs[4:]
    table = Table(table_ref, columns, slots)

    def gather(i, act):
        straight = first == (i < 2)

        def column(j, carry):
            start = table.end(i, j)

            def block(t, inner):
                k = table.slot(i, j, t)
                row, col = (k, j) if straight else (j, k)
                row = pl.ds(pl.multiple_of(row * SIDE, SIDE), SIDE)
                col = pl.ds(pl.multiple_of(col * SIDE, SIDE), SIDE)
                act(pltpu.make_async_copy(weights[i].at[row, col], bufs[i].at[start + t], gather_sems.at[i]))
                return inner

            return lax.fori_loop(0, table.end(i, j + 1) - start, block, carry)

        lax.fori_loop(0, columns, column, 0)

    def write(i, act):
        def piece(t, carry):
            where = pl.ds(t * PIECE, PIECE)
            act(pltpu.make_async_copy(bufs[i].at[where], lists.at[i, where], write_sems.at[i]))
            return carry

        lax.fori_loop(0, (table.end(i, columns) + PIECE - 1) // PIECE, piece, 0)

    for i in range(3):
        gather(i, lambda copy: copy.start())
    for i in range(3):
        gather(i, lambda copy: copy.wait())
        write(i, lambda copy: copy.start())
    for i in range(3):
        write(i, lambda copy: copy.wait())


def pack_blocks(weights, table, first, group, after):
    deep, columns = (size // SIDE for size in weights[0].shape)
    blocks = deep * columns
    if not first:
        deep, columns = columns, deep
    shape = (-(-blocks // PIECE) * PIECE + PIECE, SIDE, SIDE)
    hbm = pl.BlockSpec(memory_space=pltpu.HBM)
    return pl.pallas_call(
        functools.partial(pack_kernel, first=first, columns=columns, slots=-(-deep // group) * group, after=len(after)),
        grid_spec=pltpu.PrefetchScalarGridSpec(
            num_scalar_prefetch=1,
            grid=(1,),
            in_specs=[hbm] * 3 + [pl.BlockSpec(memory_space=pl.ANY)] * len(after),
            out_specs=hbm,
            scratch_shapes=[pltpu.VMEM(shape, BF16)] * 3 + [pltpu.SemaphoreType.DMA((3,))] * 2,
        ),
        out_shape=jax.ShapeDtypeStruct((3,) + shape, BF16),
        compiler_params=pltpu.CompilerParams(vmem_limit_bytes=48 * MIB),
        cost_estimate=BRIEF,
        name="pack_blocks",
    )(table, *weights, *after)


class Phases:
    def __init__(self, table, lists, bufs, sems, group, order):
        self.table = table
        self.lists, self.bufs, self.sems = lists, bufs, sems
        self.group, self.order = group, order
        self.half = table.columns // 2

    def copies(self, p, act):
        i, side = self.order[p]
        ring = p % len(self.bufs)
        start = self.table.end(i, side * self.half)
        total = self.table.end(i, (side + 1) * self.half) - start

        def piece(t, carry):
            act(pltpu.make_async_copy(
                self.lists.at[i, pl.ds(start + t * PIECE, PIECE)],
                self.bufs[ring].at[pl.ds(t * PIECE, PIECE)],
                self.sems.at[ring],
            ))
            return carry

        lax.fori_loop(0, (total + PIECE - 1) // PIECE, piece, 0)
        return ring, total

    def begin(self):
        for p in range(len(self.bufs)):
            self.copies(p, lambda copy: copy.start())

    def dot(self, i, j, g, first, left, buf, straight):
        group = self.group
        start = self.table.end(i, j) + g * group - first
        acts = jnp.concatenate([left[self.table.slot(i, j, g * group + s)] for s in range(group)], axis=1)
        if straight:
            block = buf[pl.ds(start, group)].reshape(group * SIDE, SIDE)
            return jnp.dot(acts, block, preferred_element_type=F32)
        block = jnp.concatenate([buf[start + s] for s in range(group)], axis=1)
        return contract_last(acts, block)

    def run(self, p, left, straight, put, add):
        i, side = self.order[p]
        ring, total = self.copies(p, lambda copy: copy.wait())
        buf = self.bufs[ring]
        buf[pl.ds(total, self.group)] = jnp.zeros((self.group, SIDE, SIDE), BF16)
        base = side * self.half
        first = self.table.end(i, base)
        for q in range(self.half):
            put(q, self.dot(i, base + q, 0, first, left, buf, straight))

        @pl.when(self.table.most(i, side) > 1)
        def _():
            def column(q, carry):
                j = base + q
                groups = (self.table.end(i, j + 1) - self.table.end(i, j) + self.group - 1) // self.group

                def more(g, inner):
                    add(q, self.dot(i, j, g, first, left, buf, straight))
                    return inner

                return lax.fori_loop(1, groups, more, carry)

            lax.fori_loop(0, self.half, column, 0)

        if p + len(self.bufs) < len(self.order):
            self.copies(p + len(self.bufs), lambda copy: copy.start())


def pre_kernel(table_ref, acts_ref, lists, *refs, after):
    refs = refs[after:]
    outs, bufs, (xs, sums, sems, own_sem, out_sems) = refs[:2], refs[2:5], refs[5:]
    blocks = acts_ref.shape[1]
    half = outs[0].shape[1]
    table = Table(table_ref, 2 * half, -(-blocks // PRE_GROUP) * PRE_GROUP)
    core = table.core()
    own = pltpu.make_async_copy(acts_ref, xs.at[:, pl.ds(0, blocks)], own_sem)
    own.start()
    order = [(i, 1 - core) for i in range(3)] + [(i, core) for i in range(3)]
    phases = Phases(table, lists, bufs, sems, PRE_GROUP, order)
    phases.begin()
    xs[:, blocks] = jnp.zeros((2,) + xs.shape[2:], BF16)
    own.wait()
    copies = []
    for p in range(6):
        i = p % 3
        left = xs.at[0] if i < 2 else xs.at[1]

        def put(q, value):
            sums[p, q] = value

        def add(q, value):
            sums[p, q] += value

        phases.run(p, left, i < 2, put, add)
        copies.append(pltpu.make_async_copy(sums.at[p], outs[p // 3].at[i], out_sems.at[p]))
        copies[-1].start()
    for copy in copies:
        copy.wait()


def pre_partials(acts, table, lists, width, after):
    _, blocks, m, _ = acts.shape
    half = width // 2 // SIDE
    anywhere = pl.BlockSpec(memory_space=pl.ANY)
    return pl.pallas_call(
        functools.partial(pre_kernel, after=len(after)),
        grid_spec=pltpu.PrefetchScalarGridSpec(
            num_scalar_prefetch=1,
            grid=(1,),
            in_specs=[anywhere, pl.BlockSpec(memory_space=pltpu.HBM)] + [anywhere] * len(after),
            out_specs=[anywhere] * 2,
            scratch_shapes=[pltpu.VMEM((blocks * half + PIECE, SIDE, SIDE), BF16)] * 3
            + [pltpu.VMEM((2, blocks + 1, m, SIDE), BF16), pltpu.VMEM((6, half, m, SIDE), F32)]
            + [pltpu.SemaphoreType.DMA((3,)), pltpu.SemaphoreType.DMA(()), pltpu.SemaphoreType.DMA((6,))],
        ),
        out_shape=[jax.ShapeDtypeStruct((3, half, m, SIDE), F32)] * 2,
        compiler_params=pltpu.CompilerParams(vmem_limit_bytes=40 * MIB),
        cost_estimate=BRIEF,
        name="pre_partials",
    )(table, acts, lists, *after)


def post_kernel(table_ref, mine_ref, other_ref, lists, *refs, after):
    refs = refs[after:]
    (keep_ref, send_ref), bufs, (hs, acc_ref, sems, own_sems) = refs[:2], refs[2:5], refs[5:]
    half, m = mine_ref.shape[1:3]
    table = Table(table_ref, keep_ref.shape[1], -(-2 * half // POST_GROUP) * POST_GROUP)
    owns = [
        pltpu.make_async_copy(ref, hs.at[:, pl.ds(n * half, half)], own_sems.at[n])
        for n, ref in enumerate((mine_ref, other_ref))
    ]
    for own in owns:
        own.start()
    order = [(2, 0), (2, 1), (0, 0), (0, 1), (1, 0), (1, 1)]
    phases = Phases(table, lists, bufs, sems, POST_GROUP, order)
    phases.begin()
    hs[:, 2 * half] = jnp.zeros((3, m, SIDE), BF16)
    for own in owns:
        own.wait()
    for p, (i, side) in enumerate(order):
        part, base = (0 if i == 2 else 1), side * phases.half

        def put(q, value):
            acc_ref[part, base + q] = value if i != 1 else acc_ref[part, base + q] + value

        def add(q, value):
            acc_ref[part, base + q] += value

        phases.run(p, hs.at[i], i == 2, put, add)
    keep_ref[...] = acc_ref[:, :, :m // 2]
    send_ref[...] = acc_ref[:, :, m // 2:].astype(BF16)


def post_partials(mine, other, table, lists, depth, after):
    _, half, m, _ = mine.shape
    blocks = depth // SIDE
    anywhere = pl.BlockSpec(memory_space=pl.ANY)
    return pl.pallas_call(
        functools.partial(post_kernel, after=len(after)),
        grid_spec=pltpu.PrefetchScalarGridSpec(
            num_scalar_prefetch=1,
            grid=(1,),
            in_specs=[anywhere] * 2 + [pl.BlockSpec(memory_space=pltpu.HBM)] + [anywhere] * len(after),
            out_specs=[pl.BlockSpec(memory_space=pltpu.VMEM)] * 2,
            scratch_shapes=[pltpu.VMEM((blocks * half + PIECE, SIDE, SIDE), BF16)] * 3
            + [pltpu.VMEM((3, 2 * half + 1, m, SIDE), BF16), pltpu.VMEM((2, blocks, m, SIDE), F32)]
            + [pltpu.SemaphoreType.DMA((3,)), pltpu.SemaphoreType.DMA((2,))],
        ),
        out_shape=[
            jax.ShapeDtypeStruct((2, blocks, m // 2, SIDE), F32),
            jax.ShapeDtypeStruct((2, blocks, m // 2, SIDE), BF16),
        ],
        compiler_params=pltpu.CompilerParams(vmem_limit_bytes=40 * MIB),
        cost_estimate=BRIEF,
        name="post_partials",
    )(table, mine, other, lists, *after)


def wgrad_kernel(first_ref, second_ref, *refs, rows, which, after):
    n = len(rows)
    acts, mines, others, refs = refs[:n], refs[n:2 * n], refs[2 * n:3 * n], refs[3 * n + after:]
    outs, (xg, hs, turned, panels, in_sems, out_sems) = refs[:len(which)], refs[len(which):]
    down = which == (2,)
    blocks, halves = xg.shape[0], hs.shape[1]
    half = halves // 2
    pre = Table(first_ref, halves, -(-blocks // PRE_GROUP) * PRE_GROUP)
    post = Table(second_ref, blocks, -(-halves // POST_GROUP) * POST_GROUP)
    core = pre.core()
    loads, start = [[], [], [], []], 0
    for c in range(n):
        span = pl.ds(start, rows[c])
        loads[3].append(pltpu.make_async_copy(acts[c].at[int(down)], xg.at[:, span], in_sems.at[3]))
        for n, i in enumerate(which):
            for ref, base in ((mines[c], 0), (others[c], half)):
                loads[i].append(pltpu.make_async_copy(ref.at[i], hs.at[n, pl.ds(base, half), span], in_sems.at[i]))
        start += rows[c]
    for i in (3,) + which:
        for load in loads[i]:
            load.start()
    for load in loads[3]:
        load.wait()
    if not down:
        for k in range(blocks):
            turned[k] = xg[k].T
        turned[blocks] = jnp.zeros(turned.shape[1:], BF16)
    turn = lambda k: lax.rem(k + half * core, halves)
    stores = []
    for n, i in enumerate(which):
        table, group, deep = (post if down else pre), WGRAD_GROUPS[i], (halves if down else blocks)
        for load in loads[i]:
            load.wait()
        if down:
            for k in range(halves):
                turned[k] = hs[0, k].T
            turned[halves] = jnp.zeros(turned.shape[1:], BF16)

        def product(panel, j, q, g):
            picks = [table.slot(i, j, g * group + t) for t in range(group)]
            right = xg[j] if down else hs[n, turn(j)]
            value = jnp.dot(jnp.concatenate([turned[k] for k in picks], axis=0), right, preferred_element_type=F32)
            for t, k in enumerate(picks):
                k = jnp.where(k < halves, turn(k), halves) if down else k
                row = pl.ds(pl.multiple_of(k * SIDE, SIDE), SIDE)
                panel[row, pl.ds(pl.multiple_of(q * SIDE, SIDE), SIDE)] = value[t * SIDE:(t + 1) * SIDE].astype(BF16)

        for base in range(0, table.columns, PANEL):
            ring = len(stores) % panels.shape[0]
            panel = panels.at[ring]
            if len(stores) >= panels.shape[0]:
                stores[-panels.shape[0]].wait()
            panel[:deep * SIDE] = jnp.zeros((deep * SIDE, PANEL * SIDE), BF16)
            for q in range(PANEL):
                product(panel, base + q, q, 0)
            most = functools.reduce(jnp.maximum, [table.end(i, base + q + 1) - table.end(i, base + q) for q in range(PANEL)])

            @pl.when(most > group)
            def _():
                def column(q, carry):
                    j = base + q
                    groups = (table.end(i, j + 1) - table.end(i, j) + group - 1) // group

                    def more(g, inner):
                        product(panel, j, q, g)
                        return inner

                    return lax.fori_loop(1, groups, more, carry)

                lax.fori_loop(0, PANEL, column, 0)

            stores.append(pltpu.make_async_copy(
                panel.at[pl.ds(0, deep * SIDE)],
                outs[n].at[:, pl.ds(base * SIDE, PANEL * SIDE)],
                out_sems.at[ring],
            ))
            stores[-1].start()
    for store in stores[-panels.shape[0]:]:
        store.wait()


def weight_grads(first, second, acts, mines, others, which, after):
    rows = [act.shape[2] for act in acts]
    tokens, blocks, halves = sum(rows), acts[0].shape[1], 2 * mines[0].shape[1]
    anywhere, hbm = pl.BlockSpec(memory_space=pl.ANY), pl.BlockSpec(memory_space=pltpu.HBM)
    shapes = [(blocks * SIDE, halves * SIDE)] * 2 + [(halves * SIDE, blocks * SIDE)]
    deep = halves if which == (2,) else blocks
    return pl.pallas_call(
        functools.partial(wgrad_kernel, rows=rows, which=which, after=len(after)),
        grid_spec=pltpu.PrefetchScalarGridSpec(
            num_scalar_prefetch=2,
            grid=(1,),
            in_specs=[anywhere] * (3 * len(acts) + len(after)),
            out_specs=[hbm] * len(which),
            scratch_shapes=[
                pltpu.VMEM((blocks, tokens, SIDE), BF16),
                pltpu.VMEM((len(which), halves, tokens, SIDE), BF16),
                pltpu.VMEM((deep + 1, SIDE, tokens), BF16),
                pltpu.VMEM((3, (deep + 1) * SIDE, PANEL * SIDE), BF16),
                pltpu.SemaphoreType.DMA((4,)),
                pltpu.SemaphoreType.DMA((3,)),
            ],
        ),
        out_shape=[jax.ShapeDtypeStruct(shapes[i], BF16) for i in which],
        compiler_params=pltpu.CompilerParams(vmem_limit_bytes=40 * MIB),
        cost_estimate=BRIEF,
        name="weight_grads",
    )(first, second, *acts, *mines, *others, *after)


def staged_body(tokens, grad_out, gate_weight, up_weight, down_weight, block_mask, *, wide):
    lines = wide // 2
    depth, width = gate_weight.shape
    core = (lax.axis_index("narrow") % 2).astype(jnp.int32).reshape(1)
    swap_core = [(i, i ^ 1) for i in range(4)]
    swap_y = [(i, i ^ 2) for i in range(4)]
    swap_x = [(i, i ^ 1) for i in range(wide)]
    fetch = lambda d: [((i + 2 * d) % wide, i) for i in range(wide)]
    give = lambda d: [(i, (i + 2 * d) % wide) for i in range(wide)]

    weights = (gate_weight, up_weight, down_weight)
    flat = jnp.stack([block_mask[0], block_mask[1], block_mask[2]])
    first = tables(flat, PRE_GROUP)
    second = tables(jnp.transpose(flat, (0, 2, 1)), POST_GROUP)
    half = width // 2 // SIDE
    turned = jnp.where(second[0] < 2 * half, (second[0] + half * core[0]) % (2 * half), second[0])
    first = flatten(*first, core)
    pre_lists = pack_blocks(weights, first, True, PRE_GROUP, [])
    straight, second = flatten(*second, core), flatten(turned, *second[1:], core)

    unit = tokens.shape[0] // sum(SHARES)
    rows = [share * unit for share in SHARES]
    blocks = depth // SIDE
    local = jnp.stack([tokens, grad_out]).reshape(2, -1, blocks, SIDE).transpose(0, 2, 1, 3)
    acts, fars = [], []
    gate = None
    for c, count in enumerate(rows):
        own = local[:, :, sum(rows[:c]):sum(rows[:c]) + count]
        if gate is not None:
            own, gate = lax.optimization_barrier((own, gate))
        far = [lax.ppermute(own, "wide", fetch(d)) for d in range(1, lines)]
        gate = far
        fars.append(far)
        if c == 0:
            post_lists = pack_blocks(weights, straight, False, POST_GROUP, [pre_lists, far[-1]])
            near = [lax.ppermute(own, "wide", swap_x)]
            rest = lax.ppermute(jnp.concatenate(far, axis=2), "wide", swap_x)
        else:
            near = []
            rest = lax.ppermute(jnp.concatenate([own] + far, axis=2), "wide", swap_x)
        acts.append(jnp.concatenate([own] + far + near + [rest], axis=2))

    count = len(rows)
    sums, arrived, sending = [None] * count, [None] * count, [None] * count
    mines, others, keeps, sends = [None] * count, [None] * count, [None] * count, [None] * count

    def before(c, after):
        send, keep = pre_partials(acts[c], first, pre_lists, width, after)
        keeps[c] = keep
        sums[c] = keep + jnp.stack([lax.ppermute(part, "narrow", swap_core) for part in send])
        sending[c] = sums[c].astype(BF16)
        arrived[c] = lax.ppermute(sending[c], "narrow", swap_y)

    def between(c):
        gate_pre, up_pre, hidden_grad = sums[c] + arrived[c].astype(F32)
        sig = jax.nn.sigmoid(gate_pre)
        hidden = gate_pre * sig * up_pre
        gate_grad = hidden_grad * up_pre * sig * (1.0 + gate_pre * (1.0 - sig))
        up_grad = hidden_grad * gate_pre * sig
        mines[c] = jnp.stack([gate_grad, up_grad, hidden]).astype(BF16)
        others[c] = lax.ppermute(mines[c], "narrow", swap_core)

    def behind(c, after):
        keep, send = post_partials(mines[c], others[c], second, post_lists, depth, after)
        keeps[c] = keep.reshape(2, blocks, lines, rows[c], SIDE)
        sends[c] = send.reshape(2, blocks, lines, rows[c], SIDE)

    def sum_pairs(group):
        keep = jnp.concatenate([keeps[c] for c in group], axis=3)
        send = jnp.concatenate([sends[c] for c in group], axis=3)
        total = keep + lax.ppermute(send, "wide", swap_x).astype(F32)
        return total[:, :, 0], [total[:, :, d].astype(BF16) for d in range(1, lines)]

    def sum_lines(final, parts):
        for d, part in enumerate(parts, 1):
            final = final + lax.ppermute(part, "wide", give(d)).astype(F32)
        return final.astype(BF16)

    before(0, [post_lists] + fars[1])
    before(1, [keeps[0]] + fars[2])
    before(2, [sending[1]])
    between(0)
    before(3, [sending[2], mines[0]])
    behind(0, [sending[3]])
    between(1)
    behind(1, [keeps[0]])
    between(2)
    behind(2, [keeps[1]])
    between(3)
    behind(3, [keeps[2]])
    (down_wgrad,) = weight_grads(first, second, acts, mines, others, (2,), [keeps[3]])
    pairs = [sum_pairs(group) for group in RETURNS]
    late = [part for _, parts in pairs[1:] for part in parts]
    gate_wgrad, up_wgrad = weight_grads(first, second, acts, mines, others, (0, 1), [down_wgrad] + late)
    finals = [sum_lines(*pair) for pair in pairs]
    both = jnp.concatenate(finals, axis=2).transpose(0, 2, 1, 3).reshape(2, -1, depth)
    return (both[0], both[1], gate_wgrad, up_wgrad, down_wgrad)


def solution(mesh):
    wide, narrow = mesh.shape["wide"], mesh.shape["narrow"]

    def body(*args):
        tokens, gate_weight = args[0], args[2]
        fits = narrow == 4 and wide == 8 and tokens.shape[0] % (4 * sum(SHARES)) == 0
        fits = fits and gate_weight.shape[1] % (PANEL * SIDE) == 0 and gate_weight.shape[0] % (PANEL * SIDE) == 0
        return staged_body(*args, wide=wide) if fits else plain_body(*args)

    return jax.shard_map(
        body,
        mesh=mesh,
        in_specs=(
            P("wide", "narrow"),
            P("wide", "narrow"),
            P("narrow", "wide"),
            P("narrow", "wide"),
            P("wide", "narrow"),
            P(None, "narrow", "wide"),
        ),
        out_specs=(
            P("wide", "narrow"),
            P("wide", "narrow"),
            P("narrow", "wide"),
            P("narrow", "wide"),
            P("wide", "narrow"),
        ),
        check_vma=False,
    )
```

```python
import functools

import jax
import jax.numpy as jnp
from jax import lax
from jax.experimental import pallas as pl
from jax.experimental.pallas import tpu as pltpu
from jax.sharding import PartitionSpec as P

F32, BF16 = jnp.float32, jnp.bfloat16
SIDE = 128
SHARES = (4, 4, 6, 2)
GATHERS = ((0,), (1,), (2,), (3,))
PRE_GROUP = 6
POST_GROUP = 8
PIECE = 8
WGRAD_GROUPS = (6, 6, 8)
PANEL = 4
PIECES = 1
MIB = 1024 * 1024
BRIEF = pl.CostEstimate(flops=1000, bytes_accessed=1000, transcendentals=0)
RETURNS = ((0, 1), (2,), (3,))


def expand_mask(blocks, height, width, dtype):
    tall = jnp.repeat(blocks, height // blocks.shape[0], axis=0)
    return jnp.repeat(tall, width // blocks.shape[1], axis=1).astype(dtype)


def contract_first(left, right):
    return lax.dot_general(
        left, right, (((0,), (0,)), ((), ())), preferred_element_type=jnp.float32
    )


def contract_last(left, right):
    return lax.dot_general(
        left, right, (((1,), (1,)), ((), ())), preferred_element_type=jnp.float32
    )


def plain_body(tokens, grad_out, gate_weight, up_weight, down_weight, block_mask):
    wtype = gate_weight.dtype
    mask_gate = expand_mask(block_mask[0], gate_weight.shape[0], gate_weight.shape[1], wtype)
    mask_up = expand_mask(block_mask[1], up_weight.shape[0], up_weight.shape[1], wtype)
    mask_down = expand_mask(block_mask[2].T, down_weight.shape[0], down_weight.shape[1], wtype)
    gate_masked = gate_weight * mask_gate
    up_masked = up_weight * mask_up
    down_masked = down_weight * mask_down
    inputs_all, cotan_all = (
        lax.all_gather(tokens, "wide", axis=0, tiled=True),
        lax.all_gather(grad_out, "wide", axis=0, tiled=True),
    )
    gate_part = jnp.dot(inputs_all, gate_masked, preferred_element_type=jnp.float32)
    up_part = jnp.dot(inputs_all, up_masked, preferred_element_type=jnp.float32)
    gate_pre, up_pre = lax.psum((gate_part, up_part), "narrow")
    sig = jax.nn.sigmoid(gate_pre)
    hidden = (gate_pre * sig * up_pre).astype(jnp.bfloat16)
    output = lax.psum_scatter(
        jnp.dot(hidden, down_masked, preferred_element_type=jnp.float32),
        "wide",
        scatter_dimension=0,
        tiled=True,
    ).astype(jnp.bfloat16)
    grad_part = contract_last(cotan_all, down_masked)
    hidden_grad = lax.psum(grad_part, "narrow")
    gate_grad = (hidden_grad * up_pre * sig * (1.0 + gate_pre * (1.0 - sig))).astype(jnp.bfloat16)
    up_grad = (hidden_grad * gate_pre * sig).astype(jnp.bfloat16)
    input_grad = lax.psum_scatter(
        contract_last(gate_grad, gate_masked) + contract_last(up_grad, up_masked),
        "wide",
        scatter_dimension=0,
        tiled=True,
    ).astype(jnp.bfloat16)
    gate_wgrad = (contract_first(inputs_all, gate_grad) * mask_gate).astype(jnp.bfloat16)
    up_wgrad = (contract_first(inputs_all, up_grad) * mask_up).astype(jnp.bfloat16)
    down_wgrad = (contract_first(hidden, cotan_all) * mask_down).astype(jnp.bfloat16)
    return (output, input_grad, gate_wgrad, up_wgrad, down_wgrad)


def tables(mask, group):
    count, columns = mask.shape[1:]
    kept = mask != 0
    before = jnp.arange(count)[:, None] < jnp.arange(count)[None, :]
    rank = jnp.sum(kept[:, :, None, :] & before[None, :, :, None], axis=1)
    slots = -(-count // group) * group
    hit = kept[:, :, None, :] & (rank[:, :, None, :] == jnp.arange(slots)[None, None, :, None])
    gap = count - jnp.arange(count)
    slot = count - jnp.sum(jnp.where(hit, gap[None, :, None, None], 0), axis=1)
    each = jnp.sum(kept, axis=1)
    earlier = jnp.arange(columns)[None, :, None] < jnp.arange(columns + 1)[None, None, :]
    ends = jnp.sum(jnp.where(earlier, each[:, :, None], 0), axis=1)
    most = (jnp.max(each.reshape(-1, 2, columns // 2), axis=2) + group - 1) // group
    slot = jnp.transpose(slot, (0, 2, 1))
    return slot.astype(jnp.int32), ends.astype(jnp.int32), most.astype(jnp.int32)


def flatten(*parts):
    return jnp.concatenate([part.reshape(-1) for part in parts])


class Table:
    def __init__(self, ref, columns, slots):
        self.ref, self.columns, self.slots = ref, columns, slots
        self.base = 3 * columns * slots

    def slot(self, i, j, s):
        return self.ref[(i * self.columns + j) * self.slots + s]

    def end(self, i, j):
        return self.ref[self.base + i * (self.columns + 1) + j]

    def most(self, i, side):
        return self.ref[self.base + 3 * (self.columns + 1) + 2 * i + side]

    def core(self):
        return self.ref[self.base + 3 * (self.columns + 1) + 6]


def pack_kernel(table_ref, *refs, first, columns, slots, after):
    weights, refs = refs[:3], refs[3 + after:]
    lists, bufs, (gather_sems, write_sems) = refs[0], refs[1:4], refs[4:]
    table = Table(table_ref, columns, slots)

    def gather(i, act):
        straight = first == (i < 2)

        def column(j, carry):
            start = table.end(i, j)

            def block(t, inner):
                k = table.slot(i, j, t)
                row, col = (k, j) if straight else (j, k)
                row = pl.ds(pl.multiple_of(row * SIDE, SIDE), SIDE)
                col = pl.ds(pl.multiple_of(col * SIDE, SIDE), SIDE)
                act(pltpu.make_async_copy(weights[i].at[row, col], bufs[i].at[start + t], gather_sems.at[i]))
                return inner

            return lax.fori_loop(0, table.end(i, j + 1) - start, block, carry)

        lax.fori_loop(0, columns, column, 0)

    def write(i, act):
        def piece(t, carry):
            where = pl.ds(t * PIECE, PIECE)
            act(pltpu.make_async_copy(bufs[i].at[where], lists.at[i, where], write_sems.at[i]))
            return carry

        lax.fori_loop(0, (table.end(i, columns) + PIECE - 1) // PIECE, piece, 0)

    for i in range(3):
        gather(i, lambda copy: copy.start())
    for i in range(3):
        gather(i, lambda copy: copy.wait())
        write(i, lambda copy: copy.start())
    for i in range(3):
        write(i, lambda copy: copy.wait())


def pack_blocks(weights, table, first, group, after):
    deep, columns = (size // SIDE for size in weights[0].shape)
    blocks = deep * columns
    if not first:
        deep, columns = columns, deep
    shape = (-(-blocks // PIECE) * PIECE + PIECE, SIDE, SIDE)
    hbm = pl.BlockSpec(memory_space=pltpu.HBM)
    return pl.pallas_call(
        functools.partial(pack_kernel, first=first, columns=columns, slots=-(-deep // group) * group, after=len(after)),
        grid_spec=pltpu.PrefetchScalarGridSpec(
            num_scalar_prefetch=1,
            grid=(1,),
            in_specs=[hbm] * 3 + [pl.BlockSpec(memory_space=pl.ANY)] * len(after),
            out_specs=hbm,
            scratch_shapes=[pltpu.VMEM(shape, BF16)] * 3 + [pltpu.SemaphoreType.DMA((3,))] * 2,
        ),
        out_shape=jax.ShapeDtypeStruct((3,) + shape, BF16),
        compiler_params=pltpu.CompilerParams(vmem_limit_bytes=48 * MIB),
        cost_estimate=BRIEF,
        name="pack_blocks",
    )(table, *weights, *after)


class Phases:
    def __init__(self, table, lists, bufs, sems, group, order):
        self.table = table
        self.lists, self.bufs, self.sems = lists, bufs, sems
        self.group, self.order = group, order
        self.half = table.columns // 2

    def copies(self, p, act):
        i, side = self.order[p]
        ring = p % len(self.bufs)
        start = self.table.end(i, side * self.half)
        total = self.table.end(i, (side + 1) * self.half) - start

        def piece(t, carry):
            act(pltpu.make_async_copy(
                self.lists.at[i, pl.ds(start + t * PIECE, PIECE)],
                self.bufs[ring].at[pl.ds(t * PIECE, PIECE)],
                self.sems.at[ring],
            ))
            return carry

        lax.fori_loop(0, (total + PIECE - 1) // PIECE, piece, 0)
        return ring, total

    def begin(self):
        for p in range(len(self.bufs)):
            self.copies(p, lambda copy: copy.start())

    def dot(self, i, j, g, first, left, buf, straight):
        group = self.group
        start = self.table.end(i, j) + g * group - first
        acts = jnp.concatenate([left[self.table.slot(i, j, g * group + s)] for s in range(group)], axis=1)
        if straight:
            block = buf[pl.ds(start, group)].reshape(group * SIDE, SIDE)
            return jnp.dot(acts, block, preferred_element_type=F32)
        block = jnp.concatenate([buf[start + s] for s in range(group)], axis=1)
        return contract_last(acts, block)

    def run(self, p, left, straight, put, add):
        i, side = self.order[p]
        ring, total = self.copies(p, lambda copy: copy.wait())
        buf = self.bufs[ring]
        buf[pl.ds(total, self.group)] = jnp.zeros((self.group, SIDE, SIDE), BF16)
        base = side * self.half
        first = self.table.end(i, base)
        for q in range(self.half):
            put(q, self.dot(i, base + q, 0, first, left, buf, straight))

        @pl.when(self.table.most(i, side) > 1)
        def _():
            def column(q, carry):
                j = base + q
                groups = (self.table.end(i, j + 1) - self.table.end(i, j) + self.group - 1) // self.group

                def more(g, inner):
                    add(q, self.dot(i, j, g, first, left, buf, straight))
                    return inner

                return lax.fori_loop(1, groups, more, carry)

            lax.fori_loop(0, self.half, column, 0)

        if p + len(self.bufs) < len(self.order):
            self.copies(p + len(self.bufs), lambda copy: copy.start())


def pre_kernel(table_ref, acts_ref, lists, *refs, after):
    refs = refs[after:]
    outs, bufs, (xs, sums, sems, own_sem, out_sems) = refs[:2], refs[2:5], refs[5:]
    blocks = acts_ref.shape[1]
    half = outs[0].shape[1]
    table = Table(table_ref, 2 * half, -(-blocks // PRE_GROUP) * PRE_GROUP)
    core = table.core()
    own = pltpu.make_async_copy(acts_ref, xs.at[:, pl.ds(0, blocks)], own_sem)
    own.start()
    order = [(i, 1 - core) for i in range(3)] + [(i, core) for i in range(3)]
    phases = Phases(table, lists, bufs, sems, PRE_GROUP, order)
    phases.begin()
    xs[:, blocks] = jnp.zeros((2,) + xs.shape[2:], BF16)
    own.wait()
    copies = []
    for p in range(6):
        i = p % 3
        left = xs.at[0] if i < 2 else xs.at[1]

        def put(q, value):
            sums[p, q] = value

        def add(q, value):
            sums[p, q] += value

        phases.run(p, left, i < 2, put, add)
        copies.append(pltpu.make_async_copy(sums.at[p], outs[p // 3].at[i], out_sems.at[p]))
        copies[-1].start()
    for copy in copies:
        copy.wait()


def pre_partials(acts, table, lists, width, after):
    _, blocks, m, _ = acts.shape
    half = width // 2 // SIDE
    anywhere = pl.BlockSpec(memory_space=pl.ANY)
    return pl.pallas_call(
        functools.partial(pre_kernel, after=len(after)),
        grid_spec=pltpu.PrefetchScalarGridSpec(
            num_scalar_prefetch=1,
            grid=(1,),
            in_specs=[anywhere, pl.BlockSpec(memory_space=pltpu.HBM)] + [anywhere] * len(after),
            out_specs=[anywhere] * 2,
            scratch_shapes=[pltpu.VMEM((blocks * half + PIECE, SIDE, SIDE), BF16)] * 3
            + [pltpu.VMEM((2, blocks + 1, m, SIDE), BF16), pltpu.VMEM((6, half, m, SIDE), F32)]
            + [pltpu.SemaphoreType.DMA((3,)), pltpu.SemaphoreType.DMA(()), pltpu.SemaphoreType.DMA((6,))],
        ),
        out_shape=[jax.ShapeDtypeStruct((3, half, m, SIDE), F32)] * 2,
        compiler_params=pltpu.CompilerParams(vmem_limit_bytes=40 * MIB),
        cost_estimate=BRIEF,
        name="pre_partials",
    )(table, acts, lists, *after)


def post_kernel(table_ref, mine_ref, other_ref, lists, *refs, after):
    refs = refs[after:]
    (keep_ref, send_ref), bufs, (hs, acc_ref, sems, own_sems) = refs[:2], refs[2:5], refs[5:]
    half, m = mine_ref.shape[1:3]
    table = Table(table_ref, keep_ref.shape[1], -(-2 * half // POST_GROUP) * POST_GROUP)
    owns = [
        pltpu.make_async_copy(ref, hs.at[:, pl.ds(n * half, half)], own_sems.at[n])
        for n, ref in enumerate((mine_ref, other_ref))
    ]
    for own in owns:
        own.start()
    order = [(2, 0), (2, 1), (0, 0), (0, 1), (1, 0), (1, 1)]
    phases = Phases(table, lists, bufs, sems, POST_GROUP, order)
    phases.begin()
    hs[:, 2 * half] = jnp.zeros((3, m, SIDE), BF16)
    for own in owns:
        own.wait()
    for p, (i, side) in enumerate(order):
        part, base = (0 if i == 2 else 1), side * phases.half

        def put(q, value):
            acc_ref[part, base + q] = value if i != 1 else acc_ref[part, base + q] + value

        def add(q, value):
            acc_ref[part, base + q] += value

        phases.run(p, hs.at[i], i == 2, put, add)
    keep_ref[...] = acc_ref[:, :, :m // 2]
    send_ref[...] = acc_ref[:, :, m // 2:].astype(BF16)


def post_partials(mine, other, table, lists, depth, after):
    _, half, m, _ = mine.shape
    blocks = depth // SIDE
    anywhere = pl.BlockSpec(memory_space=pl.ANY)
    return pl.pallas_call(
        functools.partial(post_kernel, after=len(after)),
        grid_spec=pltpu.PrefetchScalarGridSpec(
            num_scalar_prefetch=1,
            grid=(1,),
            in_specs=[anywhere] * 2 + [pl.BlockSpec(memory_space=pltpu.HBM)] + [anywhere] * len(after),
            out_specs=[pl.BlockSpec(memory_space=pltpu.VMEM)] * 2,
            scratch_shapes=[pltpu.VMEM((blocks * half + PIECE, SIDE, SIDE), BF16)] * 3
            + [pltpu.VMEM((3, 2 * half + 1, m, SIDE), BF16), pltpu.VMEM((2, blocks, m, SIDE), F32)]
            + [pltpu.SemaphoreType.DMA((3,)), pltpu.SemaphoreType.DMA((2,))],
        ),
        out_shape=[
            jax.ShapeDtypeStruct((2, blocks, m // 2, SIDE), F32),
            jax.ShapeDtypeStruct((2, blocks, m // 2, SIDE), BF16),
        ],
        compiler_params=pltpu.CompilerParams(vmem_limit_bytes=40 * MIB),
        cost_estimate=BRIEF,
        name="post_partials",
    )(table, mine, other, lists, *after)


def wgrad_kernel(first_ref, second_ref, *refs, rows, which, after):
    n = len(rows)
    acts, mines, others, refs = refs[:n], refs[n:2 * n], refs[2 * n:3 * n], refs[3 * n + after:]
    outs, (xg, hs, turned, panels, in_sems, out_sems) = refs[:len(which)], refs[len(which):]
    down = which == (2,)
    blocks, halves = xg.shape[0], hs.shape[1]
    half = halves // 2
    pre = Table(first_ref, halves, -(-blocks // PRE_GROUP) * PRE_GROUP)
    post = Table(second_ref, blocks, -(-halves // POST_GROUP) * POST_GROUP)
    core = pre.core()
    loads, start = [[], [], [], []], 0
    for c in range(n):
        span = pl.ds(start, rows[c])
        loads[3].append(pltpu.make_async_copy(acts[c].at[int(down)], xg.at[:, span], in_sems.at[3]))
        for n, i in enumerate(which):
            for ref, base in ((mines[c], 0), (others[c], half)):
                loads[i].append(pltpu.make_async_copy(ref.at[i], hs.at[n, pl.ds(base, half), span], in_sems.at[i]))
        start += rows[c]
    for i in (3,) + which:
        for load in loads[i]:
            load.start()
    for load in loads[3]:
        load.wait()
    if not down:
        for k in range(blocks):
            turned[k] = xg[k].T
        turned[blocks] = jnp.zeros(turned.shape[1:], BF16)
    turn = lambda k: lax.rem(k + half * core, halves)
    stores = []
    for n, i in enumerate(which):
        table, group, deep = (post if down else pre), WGRAD_GROUPS[i], (halves if down else blocks)
        for load in loads[i]:
            load.wait()
        if down:
            for k in range(halves):
                turned[k] = hs[0, k].T
            turned[halves] = jnp.zeros(turned.shape[1:], BF16)

        def product(panel, j, q, g):
            picks = [table.slot(i, j, g * group + t) for t in range(group)]
            right = xg[j] if down else hs[n, turn(j)]
            value = jnp.dot(jnp.concatenate([turned[k] for k in picks], axis=0), right, preferred_element_type=F32)
            for t, k in enumerate(picks):
                k = jnp.where(k < halves, turn(k), halves) if down else k
                row = pl.ds(pl.multiple_of(k * SIDE, SIDE), SIDE)
                panel[row, pl.ds(pl.multiple_of(q * SIDE, SIDE), SIDE)] = value[t * SIDE:(t + 1) * SIDE].astype(BF16)

        for base in range(0, table.columns, PANEL):
            ring = len(stores) % panels.shape[0]
            panel = panels.at[ring]
            if len(stores) >= panels.shape[0]:
                stores[-panels.shape[0]].wait()
            panel[:deep * SIDE] = jnp.zeros((deep * SIDE, PANEL * SIDE), BF16)
            for q in range(PANEL):
                product(panel, base + q, q, 0)
            most = functools.reduce(jnp.maximum, [table.end(i, base + q + 1) - table.end(i, base + q) for q in range(PANEL)])

            @pl.when(most > group)
            def _():
                def column(q, carry):
                    j = base + q
                    groups = (table.end(i, j + 1) - table.end(i, j) + group - 1) // group

                    def more(g, inner):
                        product(panel, j, q, g)
                        return inner

                    return lax.fori_loop(1, groups, more, carry)

                lax.fori_loop(0, PANEL, column, 0)

            stores.append(pltpu.make_async_copy(
                panel.at[pl.ds(0, deep * SIDE)],
                outs[n].at[:, pl.ds(base * SIDE, PANEL * SIDE)],
                out_sems.at[ring],
            ))
            stores[-1].start()
    for store in stores[-panels.shape[0]:]:
        store.wait()


def weight_grads(first, second, acts, mines, others, which, after):
    rows = [act.shape[2] for act in acts]
    tokens, blocks, halves = sum(rows), acts[0].shape[1], 2 * mines[0].shape[1]
    anywhere, hbm = pl.BlockSpec(memory_space=pl.ANY), pl.BlockSpec(memory_space=pltpu.HBM)
    shapes = [(blocks * SIDE, halves * SIDE)] * 2 + [(halves * SIDE, blocks * SIDE)]
    deep = halves if which == (2,) else blocks
    return pl.pallas_call(
        functools.partial(wgrad_kernel, rows=rows, which=which, after=len(after)),
        grid_spec=pltpu.PrefetchScalarGridSpec(
            num_scalar_prefetch=2,
            grid=(1,),
            in_specs=[anywhere] * (3 * len(acts) + len(after)),
            out_specs=[hbm] * len(which),
            scratch_shapes=[
                pltpu.VMEM((blocks, tokens, SIDE), BF16),
                pltpu.VMEM((len(which), halves, tokens, SIDE), BF16),
                pltpu.VMEM((deep + 1, SIDE, tokens), BF16),
                pltpu.VMEM((3, (deep + 1) * SIDE, PANEL * SIDE), BF16),
                pltpu.SemaphoreType.DMA((4,)),
                pltpu.SemaphoreType.DMA((3,)),
            ],
        ),
        out_shape=[jax.ShapeDtypeStruct(shapes[i], BF16) for i in which],
        compiler_params=pltpu.CompilerParams(vmem_limit_bytes=40 * MIB),
        cost_estimate=BRIEF,
        name="weight_grads",
    )(first, second, *acts, *mines, *others, *after)


def staged_body(tokens, grad_out, gate_weight, up_weight, down_weight, block_mask, *, wide):
    lines = wide // 2
    depth, width = gate_weight.shape
    core = (lax.axis_index("narrow") % 2).astype(jnp.int32).reshape(1)
    swap_core = [(i, i ^ 1) for i in range(4)]
    swap_y = [(i, i ^ 2) for i in range(4)]
    swap_x = [(i, i ^ 1) for i in range(wide)]
    fetch = lambda d: [((i + 2 * d) % wide, i) for i in range(wide)]
    give = lambda d: [(i, (i + 2 * d) % wide) for i in range(wide)]

    weights = (gate_weight, up_weight, down_weight)
    flat = jnp.stack([block_mask[0], block_mask[1], block_mask[2]])
    first = tables(flat, PRE_GROUP)
    second = tables(jnp.transpose(flat, (0, 2, 1)), POST_GROUP)
    half = width // 2 // SIDE
    turned = jnp.where(second[0] < 2 * half, (second[0] + half * core[0]) % (2 * half), second[0])
    first = flatten(*first, core)
    pre_lists = pack_blocks(weights, first, True, PRE_GROUP, [])
    straight, second = flatten(*second, core), flatten(turned, *second[1:], core)

    unit = tokens.shape[0] // sum(SHARES)
    rows = [share * unit for share in SHARES]
    blocks = depth // SIDE
    local = jnp.stack([tokens, grad_out]).reshape(2, -1, blocks, SIDE).transpose(0, 2, 1, 3)
    acts = []

    def fetch_lines(group, after=None):
        own = local[:, :, sum(rows[:group[0]]):sum(rows[:group[-1] + 1])]
        if after is not None:
            own, after = lax.optimization_barrier((own, after))
        return [own] + [lax.ppermute(own, "wide", fetch(d)) for d in range(1, lines)]

    def fetch_pairs(group, line, own_apart=False, after=None):
        own = line[0]
        sent = jnp.concatenate(line[1:] if own_apart else line, axis=2)
        if after is not None:
            sent, after = lax.optimization_barrier((sent, after))
        near = [lax.ppermute(own, "wide", swap_x)] if own_apart else []
        rest = lax.ppermute(sent, "wide", swap_x)
        deep = own.shape[2]
        line = line + near + [rest[:, :, at:at + deep] for at in range(0, rest.shape[2], deep)]
        for c in group:
            at = sum(rows[group[0]:c])
            acts.append(jnp.concatenate([part[:, :, at:at + rows[c]] for part in line], axis=2))

    line = fetch_lines(GATHERS[0])
    post_lists = pack_blocks(weights, straight, False, POST_GROUP, [pre_lists, line[-1]])
    fetch_pairs(GATHERS[0], line, own_apart=True)
    following = fetch_lines(GATHERS[1], line[1:])
    fetch_pairs(GATHERS[1], following)

    count = len(rows)
    sums, arrived, sending = [None] * count, [None] * count, [None] * count
    mines, others, keeps, sends = [None] * count, [None] * count, [None] * count, [None] * count

    def exchange(send):
        cut = half // PIECES
        parts = [part[at:at + cut] for part in send for at in range(0, half, cut)]
        return jnp.concatenate([lax.ppermute(part, "narrow", swap_core) for part in parts]).reshape(send.shape)

    def before(c, after):
        send, keep = pre_partials(acts[c], first, pre_lists, width, after)
        keeps[c] = keep
        sums[c] = keep + exchange(send)
        sending[c] = sums[c].astype(BF16)
        arrived[c] = lax.ppermute(sending[c], "narrow", swap_y)

    def between(c):
        gate_pre, up_pre, hidden_grad = sums[c] + arrived[c].astype(F32)
        sig = jax.nn.sigmoid(gate_pre)
        hidden = gate_pre * sig * up_pre
        gate_grad = hidden_grad * up_pre * sig * (1.0 + gate_pre * (1.0 - sig))
        up_grad = hidden_grad * gate_pre * sig
        mines[c] = jnp.stack([gate_grad, up_grad, hidden]).astype(BF16)
        others[c] = lax.ppermute(mines[c], "narrow", swap_core)

    def behind(c, after):
        keep, send = post_partials(mines[c], others[c], second, post_lists, depth, after)
        keeps[c] = keep.reshape(2, blocks, lines, rows[c], SIDE)
        sends[c] = send.reshape(2, blocks, lines, rows[c], SIDE)

    def sum_pairs(group):
        keep = jnp.concatenate([keeps[c] for c in group], axis=3)
        send = jnp.concatenate([sends[c] for c in group], axis=3)
        total = keep + lax.ppermute(send, "wide", swap_x).astype(F32)
        return total[:, :, 0], [total[:, :, d].astype(BF16) for d in range(1, lines)]

    def sum_lines(final, parts):
        for d, part in enumerate(parts, 1):
            final = final + lax.ppermute(part, "wide", give(d)).astype(F32)
        return final.astype(BF16)

    before(0, [post_lists] + following[1:])
    line = fetch_lines(GATHERS[2], following[1:])
    before(1, [keeps[0]])
    fetch_pairs(GATHERS[2], line, after=sending[0])
    before(2, [sending[1]])
    line = fetch_lines(GATHERS[3], sending[2])
    fetch_pairs(GATHERS[3], line)
    between(0)
    before(3, [sending[2], mines[0]])
    behind(0, [sending[3]])
    between(1)
    behind(1, [keeps[0]])
    between(2)
    behind(2, [keeps[1]])
    between(3)
    behind(3, [keeps[2]])
    keeps[0], keeps[2] = lax.optimization_barrier((keeps[0], keeps[2]))
    (down_wgrad,) = weight_grads(first, second, acts, mines, others, (2,), [keeps[3]])
    pairs = [sum_pairs(group) for group in RETURNS]
    late = [part for _, parts in pairs[1:] for part in parts]
    gate_wgrad, up_wgrad = weight_grads(first, second, acts, mines, others, (0, 1), [down_wgrad] + late)
    finals = [sum_lines(*pair) for pair in pairs]
    both = jnp.concatenate(finals, axis=2).transpose(0, 2, 1, 3).reshape(2, -1, depth)
    return (both[0], both[1], gate_wgrad, up_wgrad, down_wgrad)


def solution(mesh):
    wide, narrow = mesh.shape["wide"], mesh.shape["narrow"]

    def body(*args):
        tokens, gate_weight = args[0], args[2]
        fits = narrow == 4 and wide == 8 and tokens.shape[0] % (4 * sum(SHARES)) == 0
        fits = fits and gate_weight.shape[1] % (PANEL * SIDE) == 0 and gate_weight.shape[0] % (PANEL * SIDE) == 0
        return staged_body(*args, wide=wide) if fits else plain_body(*args)

    return jax.shard_map(
        body,
        mesh=mesh,
        in_specs=(
            P("wide", "narrow"),
            P("wide", "narrow"),
            P("narrow", "wide"),
            P("narrow", "wide"),
            P("wide", "narrow"),
            P(None, "narrow", "wide"),
        ),
        out_specs=(
            P("wide", "narrow"),
            P("wide", "narrow"),
            P("narrow", "wide"),
            P("narrow", "wide"),
            P("wide", "narrow"),
        ),
        check_vma=False,
    )
```
